256 devices in a mesh: cluster: 64 (over z, y, core), sub: 4 (over x).
Axes of the slice: x: 4, y: 4, z: 8, core: 2. Of those that a mesh axis runs over, the one named last changes fastest.
Arguments:
- adjoint_input: bfloat16 [1024, 2, 4, 128], P('cluster'), may hold values from -6 to 6
- efie_left: bfloat16 [1024, 8, 2, 64, 128], P('cluster', None, None, 'sub'), may hold values from -0.375 to 0.375
- efie_right: bfloat16 [1024, 8, 2, 64, 128], P('cluster', None, None, 'sub'), may hold values from -0.1875 to 0.1875
- dual_left: bfloat16 [1024, 8, 2, 64, 128], P('cluster', None, None, 'sub'), may hold values from -0.375 to 0.375
- dual_right: bfloat16 [1024, 8, 2, 64, 128], P('cluster', None, None, 'sub'), may hold values from -0.1875 to 0.1875
- block_ranks: int32 [1024, 8], P('cluster'), may hold values from 16 to 64
- far_cols: int32 [1024, 8], P('cluster'), may hold values from 0 to 1023, as said below
- efie_near: bfloat16 [1024, 8, 2, 128, 128], P('cluster', 'sub'), may hold values from -0.125 to 0.125
- dual_near: bfloat16 [1024, 8, 2, 128, 128], P('cluster', 'sub'), may hold values from -0.125 to 0.125
- near_cols: int32 [1024, 8], P('cluster', 'sub'), may hold values from 0 to 1023, as said below
Outputs:
- adjoint_efie: bfloat16 [1024, 2, 4, 128], P('cluster', None, 'sub')
- adjoint_dual: bfloat16 [1024, 2, 4, 128], P('cluster', None, 'sub')
The draws below stay inside these ranges and needn't reach their ends.
Inputs may be any that keep to these rules, and one draw needn't show every extreme that they name: `far_cols`: the clusters e * 16 to e * 16 + 15 belong to index e of cluster; among the far blocks of the 16 block rows of one index, at most 4 have column clusters of any one index. `near_cols`: entry k of row i lies within 16 of i, and entry 0 of each row is i itself.
All inputs are finite; a program needn't handle non-finite values.
Results may differ from the reference program's by a relative error of at most 0.0035.
Values sent between devices are 32-bit elements; how exact they have to be, the bound alone decides.
No kernel may reach another device: no remote copies, remote signals or barrier semaphores. Data moves between devices by JAX's collectives and lax.ppermute only.
A program may use at most 64 MiB of HBM per device.

```python
import jax
import jax.numpy as jnp
from jax import lax

CS = 128
R = 64
NV = 4
CPD = 16
FAR = 8
NEAR = 8
CAP = 4
CLUSTERS = 1024
N_CLUSTER = 64


def draw_far_cols(key, part):
    key = jax.random.fold_in(key, 11)
    subkeys = jax.random.split(key, 5)
    devices = N_CLUSTER
    capacity = CAP
    per_row = CPD * FAR
    pool_size = devices * capacity
    multiple = capacity - jax.random.randint(subkeys[0], (devices,), 0, capacity // 2 + 1)
    chosen = jax.random.randint(subkeys[1], (devices,), 0, devices)
    pool_ids = jnp.arange(pool_size, dtype=jnp.int32)
    pool_dest = pool_ids // capacity
    pool_copy = pool_ids % capacity
    forced = pool_dest[None, :] == chosen[:, None]
    usable = forced | (pool_copy[None, :] < multiple[pool_dest][None, :])
    scores = jax.random.randint(subkeys[2], (devices, pool_size), 0, 1 << 20)
    scores = jnp.where(forced, 0, jnp.where(usable, scores + 1, (1 << 20) + 2))
    ranked = jnp.argsort(scores * pool_size + pool_ids[None, :], axis=1)[:, :per_row]
    dest_dev = ranked // capacity
    shuffle = jnp.argsort(jax.random.randint(subkeys[3], (devices, per_row), 0, 1 << 20) * per_row + jnp.arange(per_row, dtype=jnp.int32)[None, :], axis=1)
    dest_dev = jnp.take_along_axis(dest_dev, shuffle, axis=1)
    local_ids = jax.random.randint(subkeys[4], (devices, per_row), 0, CPD)
    return (dest_dev * CPD + local_ids).reshape(devices * CPD, FAR).astype(jnp.int32)


def draw_block_ranks(key, part):
    key = jax.random.fold_in(key, 23)
    key_one, key_two = jax.random.split(key)
    values = jax.random.randint(key_one, (CLUSTERS, FAR), R // 4, R + 1)
    marked = jax.random.randint(key_two, (), 0, CLUSTERS * FAR)
    flat_ids = jnp.arange(CLUSTERS * FAR, dtype=jnp.int32).reshape(CLUSTERS, FAR)
    return jnp.where(flat_ids == marked, R, values).astype(jnp.int32)


def draw_near_cols(key, part):
    key = jax.random.fold_in(key, 37)
    offsets = jax.random.randint(key, (CLUSTERS, NEAR), -CPD, CPD + 1)
    slot_ids = jnp.arange(NEAR, dtype=jnp.int32)[None, :]
    offsets = jnp.where(slot_ids == 0, 0, offsets)
    row_ids = jnp.arange(CLUSTERS, dtype=jnp.int32)[:, None]
    return jnp.clip(row_ids + offsets, 0, CLUSTERS - 1).astype(jnp.int32)


def steps_of(rng, extent, cuts, smallest, largest):
    def one(axis_at, parts):
        heights = jax.random.uniform(jax.random.fold_in(jax.random.fold_in(rng, 6), axis_at), (parts,), jnp.float32, smallest / len(cuts), largest / len(cuts))
        return jnp.repeat(jnp.exp(heights), extent[axis_at] // parts).reshape((-1,) + (1,) * (len(extent) - axis_at - 1))

    gain = one(*cuts[0])
    for cut in cuts[1:]:
        gain = gain * one(*cut)
    return gain


def normal_values(key, shape, deviation, reach, cuts=(), kind=jnp.bfloat16):
    values = jax.random.normal(key, shape, jnp.float32) * deviation
    if len(cuts) > 0:
        values = steps_of(key, shape, cuts, -0.22, 0.18) * values
    return jnp.clip(values, min=-reach, max=reach).astype(kind)


def setup_inputs(seed: int = 0) -> dict:
    streams_of = jax.random.split(jax.random.key(seed), 11)
    return {
        "adjoint_input": normal_values(streams_of[0], (CLUSTERS, 2, NV, CS), 1.0, 6.0, ((0, 64),)),
        "efie_left": normal_values(streams_of[1], (CLUSTERS, FAR, 2, R, CS), (2 * CS) ** -0.5, 0.375, ((0, 64), (3, 4))),
        "efie_right": normal_values(streams_of[2], (CLUSTERS, FAR, 2, R, CS), (2 * R * FAR) ** -0.5, 0.1875, ((0, 64), (3, 4))),
        "dual_left": normal_values(streams_of[3], (CLUSTERS, FAR, 2, R, CS), (2 * CS) ** -0.5, 0.375, ((0, 64), (3, 4))),
        "dual_right": normal_values(streams_of[4], (CLUSTERS, FAR, 2, R, CS), (2 * R * FAR) ** -0.5, 0.1875, ((0, 64), (3, 4))),
        "block_ranks": draw_block_ranks(jax.random.fold_in(streams_of[10], 71), 0),
        "far_cols": draw_far_cols(jax.random.fold_in(streams_of[10], 71), 0),
        "efie_near": normal_values(streams_of[7], (CLUSTERS, NEAR, 2, CS, CS), (2 * CS * NEAR) ** -0.5, 0.125, ((0, 64), (1, 4))),
        "dual_near": normal_values(streams_of[8], (CLUSTERS, NEAR, 2, CS, CS), (2 * CS * NEAR) ** -0.5, 0.125, ((0, 64), (1, 4))),
        "near_cols": draw_near_cols(jax.random.fold_in(streams_of[10], 71), 0),
    }


def conj_apply(mat_real, mat_imag, vec_real, vec_imag, pattern):
    def product(matrix, vector):
        return jnp.einsum(pattern, matrix, vector, precision=lax.Precision.HIGHEST)
    return (product(mat_real, vec_real) + product(mat_imag, vec_imag),
            product(mat_real, vec_imag) - product(mat_imag, vec_real))


def plain_apply(mat_real, mat_imag, vec_real, vec_imag, pattern):
    def product(matrix, vector):
        return jnp.einsum(pattern, matrix, vector, precision=lax.Precision.HIGHEST)
    return (product(mat_real, vec_real) - product(mat_imag, vec_imag),
            product(mat_real, vec_imag) + product(mat_imag, vec_real))


def reference(adjoint_input, efie_left, efie_right, dual_left, dual_right, block_ranks, far_cols, efie_near, dual_near, near_cols):
    columns = jnp.arange(R, dtype=jnp.int32)

    def far_terms(left_factor, right_factor, vectors, row_ranks):
        left_factor = left_factor.astype(jnp.float32)
        right_factor = right_factor.astype(jnp.float32)
        coef_real, coef_imag = conj_apply(left_factor[:, 0], left_factor[:, 1], vectors[0], vectors[1], "frs,ns->fnr")
        keep_mask = columns[None, None, :] < row_ranks[:, None, None]
        coef_real = lax.optimization_barrier(jnp.where(keep_mask, coef_real, 0.0).astype(jnp.bfloat16)).astype(jnp.float32)
        coef_imag = lax.optimization_barrier(jnp.where(keep_mask, coef_imag, 0.0).astype(jnp.bfloat16)).astype(jnp.float32)
        out_real, out_imag = plain_apply(right_factor[:, 0], right_factor[:, 1], coef_real, coef_imag, "frt,fnr->fnt")
        return jnp.stack([out_real, out_imag], 1)

    def near_terms(blocks, vectors):
        blocks = blocks.astype(jnp.float32)
        out_real, out_imag = conj_apply(blocks[:, 0], blocks[:, 1], vectors[0], vectors[1], "kst,ns->knt")
        return jnp.stack([out_real, out_imag], 1)

    def visit_cluster(totals, cluster_id):
        vectors = adjoint_input[cluster_id].astype(jnp.float32)
        row_ranks = block_ranks[cluster_id]
        far_part = jnp.stack([far_terms(efie_left[cluster_id], efie_right[cluster_id], vectors, row_ranks),
                              far_terms(dual_left[cluster_id], dual_right[cluster_id], vectors, row_ranks)], 1)
        near_part = jnp.stack([near_terms(efie_near[cluster_id], vectors),
                               near_terms(dual_near[cluster_id], vectors)], 1)
        totals = totals.at[far_cols[cluster_id]].add(far_part)
        totals = totals.at[near_cols[cluster_id]].add(near_part)
        return totals, None

    start_sum = jnp.zeros((CLUSTERS, 2, 2, NV, CS), jnp.float32)
    totals, _ = lax.scan(visit_cluster, start_sum, jnp.arange(CLUSTERS, dtype=jnp.int32))
    result = totals.astype(jnp.bfloat16)
    return result[:, 0], result[:, 1]
```

```python
import jax
import jax.numpy as jnp
from jax import lax
from jax.experimental import pallas as pl
from jax.experimental.pallas import tpu as pltpu
from jax.sharding import PartitionSpec as P

F32 = jnp.float32
BF16 = jnp.bfloat16
LIMIT = 48 * 1024 * 1024


def iota(shape, dim):
    return lax.broadcasted_iota(jnp.int32, shape, dim)


def dot(left, right, dims=((1,), (0,))):
    return lax.dot_general(left, right, (dims, ((), ())), preferred_element_type=F32)


def vectors(x, me, cluster, copies):
    rows = 8 * copies
    shape = (2 * rows, x.shape[0])
    row, col = iota(shape, 0), iota(shape, 1)
    half = row // rows
    part = (row // copies) % 2
    vec = (me + (row % rows) // (2 * copies)) & 3
    wanted = cluster * 8 + jnp.where(half == part, 0, 1) * 4 + vec
    sign = jnp.where((half == 1) & (part == 1), -1.0, 1.0)
    both = dot(jnp.where(col == wanted, sign, 0.0).astype(BF16), x)
    return jnp.concatenate([both[:rows], both[rows:]], axis=1).astype(BF16)


def far_kernel(me_ref, rank_ref, x_ref, le, re, ld, rd, *outs):
    per_step = le.shape[0]
    step = pl.program_id(0)
    me = me_ref[0]
    x = x_ref[...]
    lane, sublane = iota((8, 128), 1), iota((8, 128), 0)
    for at in range(per_step):
        cluster = step * per_step + at
        lhs = vectors(x, me, cluster, 8)
        ranks = jnp.zeros((8, 128), jnp.int32)
        for f in range(8):
            ranks = jnp.where(lane // 16 == f, rank_ref[cluster, f], ranks)
        keep = (lane // 16 == sublane) & (me * 16 + lane % 16 < ranks)
        for op, (left, right) in enumerate(((le, re), (ld, rd))):
            u = jnp.concatenate([left[at, :, q].reshape(128, 128) for q in (0, 1)], axis=1)
            coef = dot(lhs, u, ((1,), (1,)))
            real = [jnp.where(keep, coef[k * 16 : k * 16 + 8], 0.0) for k in range(4)]
            imag = [jnp.where(keep, coef[k * 16 + 8 : k * 16 + 16], 0.0) for k in range(4)]
            first = jnp.concatenate([v for k in range(4) for v in (real[k], imag[k])], axis=0)
            second = jnp.concatenate([v for k in range(4) for v in (-imag[k], real[k])], axis=0)
            spread = jnp.concatenate([first, second], axis=1).astype(BF16)
            v = jnp.concatenate([right[at, :, q].reshape(128, 128) for q in (0, 1)], axis=0)
            far = dot(spread, v)
            for k in range(4):
                for q in range(2):
                    start = k * 16 + q * 8
                    outs[k][op * 2 + q, at * 8 : at * 8 + 8, :] = far[start : start + 8]


def near_kernel(me_ref, col_ref, x_ref, de, dd, low, mid, high, window):
    per_step = de.shape[0]
    step = pl.program_id(0)
    me, base = me_ref[0], me_ref[1]
    x = x_ref[...]

    @pl.when(step == 0)
    def _():
        window[...] = jnp.zeros_like(window)

    for at in range(per_step):
        cluster = step * per_step + at
        lhs = vectors(x, me, cluster, 1)
        for slot in range(2):
            d = jnp.concatenate([r[at, slot].reshape(256, 128) for r in (de, dd)], axis=1)
            out = dot(lhs, d)
            target = col_ref[cluster, slot] - base
            window[target, 0] += out[:, :128]
            window[target, 1] += out[:, 128:]

    @pl.when(step == pl.num_programs(0) - 1)
    def _():
        low[...] = window[0:16]
        mid[...] = window[16:32]
        high[...] = window[32:48]


def merge_kernel(mid, left, right, *outs):
    for k in range(4):
        for j in range(4):
            rows = pl.ds((j // 2) * 8 + k * 2 + j % 2, 16, stride=16)
            outs[k][j] = mid[rows, :] + left[rows, :] + right[rows, :]


def halves(value):
    high = value.astype(BF16)
    return high, (value - high.astype(F32)).astype(BF16)


def send_kernel(slot_ref, cols_ref, a, b, c, d, out):
    slot = jnp.broadcast_to(slot_ref[0:1, :], (64, 128))
    target = iota((64, 128), 0)
    picks = [jnp.where(slot == target * 4 + k, 1.0, 0.0).astype(BF16) for k in range(4)]
    pick = jnp.concatenate(picks, axis=0)
    pick = jnp.concatenate([pick, pick], axis=1)
    for pair in range(2):
        parts = []
        for j in (pair * 2, pair * 2 + 1):
            high, low = halves(a[j] + b[j] + c[j] + d[j])
            parts.append(jnp.concatenate([high, low], axis=0))
        moved = dot(pick, jnp.concatenate(parts, axis=1))
        for q in range(2):
            for k in range(4):
                rows = pl.ds(k * 4 + pair * 2 + q, 64, stride=17)
                out[rows, :] = moved[k * 64 : k * 64 + 64, q * 128 : q * 128 + 128]
    here = jnp.where(slot // 4 == target, 1.0, 0.0).astype(BF16)
    place = jnp.where(cols_ref[...] == iota((128, 128), 1), 1.0, 0.0).astype(BF16)
    out[pl.ds(16, 64, stride=17), :] = dot(here, place)


def sum_kernel(got, na, nb, nc, nd, efie, dual):
    marks = got[pl.ds(16, 64, stride=17), :].T
    pick = jnp.concatenate([marks[k * 16 : k * 16 + 16, :] for k in range(4)], axis=1).astype(BF16)
    pick = jnp.concatenate([pick, pick], axis=1)
    sums = []
    for j in range(4):
        value = jnp.concatenate([got[pl.ds(k * 4 + j, 64, stride=17), :] for k in range(4)], axis=0)
        high, low = halves(value)
        far = dot(pick, jnp.concatenate([high, low], axis=0))
        sums.append(far + na[j] + nb[j] + nc[j] + nd[j])
    efie[...] = jnp.stack([sums[0], sums[1]], axis=1).astype(BF16)
    dual[...] = jnp.stack([sums[2], sums[3]], axis=1).astype(BF16)


def whole(shape):
    return pl.BlockSpec(shape, lambda *_: (0,) * len(shape))


SMEM = pl.BlockSpec(memory_space=pltpu.SMEM)
VMEM = pl.BlockSpec(memory_space=pltpu.VMEM)


def per_device(
    adjoint_input,
    efie_left,
    efie_right,
    dual_left,
    dual_right,
    block_ranks,
    far_cols,
    efie_near,
    dual_near,
    near_cols,
):
    per_dev = adjoint_input.shape[0]
    subs = lax.axis_size("sub")
    position = lax.axis_index("cluster")
    me = lax.axis_index("sub")
    scalars = jnp.stack([me, position * per_dev - per_dev]).astype(jnp.int32)
    x = adjoint_input.reshape(per_dev * 8, 128)
    params = pltpu.CompilerParams(vmem_limit_bytes=LIMIT)

    def struct(shape, dtype=F32):
        return jax.ShapeDtypeStruct(shape, dtype)

    step = 4
    far_block = pl.BlockSpec((step, 8, 2, 16, 128), lambda i: (i, 0, 0, 0, 0))
    far = pl.pallas_call(
        far_kernel,
        grid=(per_dev // step,),
        in_specs=[SMEM, SMEM, whole((128, 128))] + [far_block] * 4,
        out_specs=[pl.BlockSpec((4, step * 8, 128), lambda i: (0, i, 0))] * 4,
        out_shape=[struct((4, 128, 128))] * 4,
        compiler_params=params,
        cost_estimate=pl.CostEstimate(flops=200_000_000, bytes_accessed=5_300_000, transcendentals=0),
        name="far",
    )(scalars, block_ranks, x, efie_left, efie_right, dual_left, dual_right)

    def shift(k):
        return [(i, (i + k) % subs) for i in range(subs)]

    far_got = [far[0]] + [lax.ppermute(far[k], "sub", shift(k)) for k in (1, 2, 3)]

    near_block = pl.BlockSpec((step, 2, 2, 128, 128), lambda i: (i, 0, 0, 0, 0))
    low, mid, high = pl.pallas_call(
        near_kernel,
        grid=(per_dev // step,),
        in_specs=[SMEM, SMEM, whole((128, 128)), near_block, near_block],
        out_specs=[whole((per_dev, 2, 8, 128))] * 3,
        out_shape=[struct((per_dev, 2, 8, 128))] * 3,
        scratch_shapes=[pltpu.VMEM((3 * per_dev, 2, 8, 128), F32)],
        compiler_params=params,
        cost_estimate=pl.CostEstimate(flops=200_000_000, bytes_accessed=4_600_000, transcendentals=0),
        name="near",
    )(scalars, near_cols, x, efie_near, dual_near)
    count = lax.axis_size("cluster")
    forward = [(i, i + 1) for i in range(count - 1)]
    backward = [(i + 1, i) for i in range(count - 1)]
    from_left = lax.ppermute(high, "cluster", forward)
    from_right = lax.ppermute(low, "cluster", backward)
    near = pl.pallas_call(
        merge_kernel,
        in_specs=[VMEM] * 3,
        out_specs=[VMEM] * 4,
        out_shape=[struct((4, per_dev, 128))] * 4,
        compiler_params=params,
        name="merge",
    )(*(v.reshape(per_dev * 16, 128) for v in (mid, from_left, from_right)))
    near_got = [near[0]] + [lax.ppermute(near[k], "sub", shift(k)) for k in (1, 2, 3)]

    cols = far_cols.reshape(-1)
    owner = cols // per_dev
    earlier = (owner[:, None] == owner[None, :]) & (jnp.arange(128)[None, :] < jnp.arange(128)[:, None])
    order = jnp.sum(earlier.astype(jnp.int32), axis=1)
    slot = jnp.broadcast_to((owner * 4 + order)[None, :], (8, 128))
    place = jnp.broadcast_to((order * 16 + cols % per_dev)[:, None], (128, 128))
    sent = pl.pallas_call(
        send_kernel,
        in_specs=[VMEM] * 6,
        out_specs=VMEM,
        out_shape=struct((count * 17, 128)),
        compiler_params=params,
        name="send",
    )(slot, place, *far_got)
    got = lax.all_to_all(sent.reshape(count * 17, 1, 128), "cluster", 0, 0, tiled=True)
    efie, dual = pl.pallas_call(
        sum_kernel,
        in_specs=[VMEM] * 5,
        out_specs=[VMEM] * 2,
        out_shape=[struct((per_dev, 2, 128), BF16)] * 2,
        compiler_params=params,
        name="total",
    )(got.reshape(count * 17, 128), *near_got)
    shape = (per_dev, 2, 1, 128)
    return efie.reshape(shape), dual.reshape(shape)


def solution(mesh):
    return jax.shard_map(
        per_device,
        mesh=mesh,
        in_specs=(
            P("cluster", None, None, None),
            P("cluster", None, None, "sub", None),
            P("cluster", None, None, "sub", None),
            P("cluster", None, None, "sub", None),
            P("cluster", None, None, "sub", None),
            P("cluster", None),
            P("cluster", None),
            P("cluster", "sub", None, None, None),
            P("cluster", "sub", None, None, None),
            P("cluster", "sub"),
        ),
        out_specs=(P("cluster", None, "sub", None), P("cluster", None, "sub", None)),
        check_vma=False,
    )
```

```python
import functools

import jax
import jax.numpy as jnp
from jax import lax
from jax.experimental import pallas as pl
from jax.experimental.pallas import tpu as pltpu
from jax.sharding import PartitionSpec as P

F32 = jnp.float32
BF16 = jnp.bfloat16
MIB = 1024 * 1024


def iota(shape, dim):
    return lax.broadcasted_iota(jnp.int32, shape, dim)


def dot(left, right, dims=((1,), (0,))):
    return lax.dot_general(left, right, (dims, ((), ())), preferred_element_type=F32)


def vectors(x, me, cluster, copies):
    rows = 8 * copies
    shape = (2 * rows, x.shape[0])
    row, col = iota(shape, 0), iota(shape, 1)
    half = row // rows
    part = (row // copies) % 2
    vec = (me + (row % rows) // (2 * copies)) & 3
    wanted = cluster * 8 + jnp.where(half == part, 0, 1) * 4 + vec
    sign = jnp.where((half == 1) & (part == 1), -1.0, 1.0)
    both = dot(jnp.where(col == wanted, sign, 0.0).astype(BF16), x)
    return jnp.concatenate([both[:rows], both[rows:]], axis=1).astype(BF16)


def planes(ref, at, axis):
    return jnp.concatenate([ref[at, :, q].reshape(128, 128) for q in (0, 1)], axis=axis)


def far_kernel(chunk, me_ref, rank_ref, x_ref, le, re, ld, rd, o0, o1, o2, o3, ble, bre, bld, brd, made, lhs, sems, out_sems):
    outs = (o0, o1, o2, o3)
    clusters = ble.shape[0]
    steps = clusters // chunk

    def loads(i):
        part = pl.ds(i * chunk, chunk)
        pairs = ((le, ble), (ld, bld), (re, bre), (rd, brd))
        return [pltpu.make_async_copy(a.at[part], b.at[part], sems.at[j, i]) for j, (a, b) in enumerate(pairs)]

    def stores(i):
        part = pl.ds(i * chunk * 8, chunk * 8)
        return [pltpu.make_async_copy(made.at[k, :, part], outs[k].at[:, part], out_sems.at[k, i]) for k in (2, 1, 3, 0)]

    for i in range(steps):
        for copy in loads(i):
            copy.start()
    me = me_ref[0]
    x = x_ref[...]
    lane, sublane = iota((8, 128), 1), iota((8, 128), 0)
    for cluster in range(clusters):
        lhs[cluster] = vectors(x, me, cluster, 8)

    def spread(coef, keep):
        rows = [jnp.where(keep, coef[k * 8 : k * 8 + 8], 0.0) for k in range(8)]
        turned = [v for k in range(4) for v in (-rows[2 * k + 1], rows[2 * k])]
        both = [jnp.concatenate(rows, axis=0), jnp.concatenate(turned, axis=0)]
        return jnp.concatenate(both, axis=1).astype(BF16)

    for i in range(steps):
        for copy in loads(i):
            copy.wait()
        for cluster in range(i * chunk, i * chunk + chunk):
            ranks = jnp.zeros((8, 128), jnp.int32)
            for f in range(8):
                ranks = jnp.where(lane // 16 == f, rank_ref[f, cluster], ranks)
            keep = (lane // 16 == sublane) & (me * 16 + lane % 16 < ranks)
            u = jnp.concatenate([planes(ble, cluster, 1), planes(bld, cluster, 1)], axis=0)
            coef = dot(lhs[cluster], u, ((1,), (1,)))
            mixed = jnp.concatenate([spread(coef[:, :128], keep), spread(coef[:, 128:], keep)], axis=0)
            v = jnp.concatenate([planes(bre, cluster, 0), planes(brd, cluster, 0)], axis=1)
            far = dot(mixed, v)
            for op in range(2):
                for k in range(4):
                    for q in range(2):
                        start = op * 64 + k * 16 + q * 8
                        made[k, op * 2 + q, cluster * 8 : cluster * 8 + 8, :] = far[
                            start : start + 8, op * 128 : op * 128 + 128
                        ]
        for copy in stores(i):
            copy.start()
    for i in range(steps):
        for copy in stores(i):
            copy.wait()


def near_kernel(chunk, me_ref, base_ref, col_ref, x_ref, de, dd, after, mid, pair, other, bde, bdd, window, sems):
    clusters = bde.shape[0]
    steps = clusters // chunk

    def loads(i):
        part = pl.ds(i * chunk, chunk)
        pairs = ((de, bde), (dd, bdd))
        return [pltpu.make_async_copy(a.at[part], b.at[part], sems.at[j, i]) for j, (a, b) in enumerate(pairs)]

    for i in range(steps):
        for copy in loads(i):
            copy.start()
    me, base = me_ref[0], base_ref[0]
    x = x_ref[...]
    window[...] = jnp.zeros_like(window)
    lhs = [vectors(x, me, cluster, 1) for cluster in range(clusters)]
    for i in range(steps):
        for copy in loads(i):
            copy.wait()
        for cluster in range(i * chunk, i * chunk + chunk):
            for slot in range(2):
                d = jnp.concatenate([r[cluster, slot].reshape(256, 128) for r in (bde, bdd)], axis=1)
                out = dot(lhs[cluster], d)
                target = col_ref[slot, cluster] - base
                window[target, 0] += out[:, :128]
                window[target, 1] += out[:, 128:]
    odd = (base // 16) & 1 == 0
    mid[...] = window[16:32]
    pair[...] = window[pl.ds(jnp.where(odd, 0, 32), 16)]
    other[...] = window[pl.ds(jnp.where(odd, 32, 0), 16)]


def halves(value):
    high = value.astype(BF16)
    return high, (value - high.astype(F32)).astype(BF16)


def send_kernel(slot_ref, cols_ref, a, b, c, d, mid, pair, other, out, *near):
    slot = jnp.broadcast_to(slot_ref[0:1, :], (64, 128))
    target = iota((64, 128), 0)
    picks = [jnp.where(slot == target * 4 + k, 1.0, 0.0).astype(BF16) for k in range(4)]
    pick = jnp.concatenate(picks, axis=0)
    pick = jnp.concatenate([pick, pick], axis=1)
    for half in range(2):
        parts = []
        for j in (half * 2, half * 2 + 1):
            high, low = halves(a[j] + b[j] + c[j] + d[j])
            parts.append(jnp.concatenate([high, low], axis=0))
        moved = dot(pick, jnp.concatenate(parts, axis=1))
        for q in range(2):
            for k in range(4):
                rows = pl.ds(k * 4 + half * 2 + q, 64, stride=17)
                out[rows, :] = moved[k * 64 : k * 64 + 64, q * 128 : q * 128 + 128]
    here = jnp.where(slot // 4 == target, 1.0, 0.0).astype(BF16)
    place = jnp.where(cols_ref[...] == iota((128, 128), 1), 1.0, 0.0).astype(BF16)
    out[pl.ds(16, 64, stride=17), :] = dot(here, place)
    for k in range(4):
        for j in range(4):
            rows = pl.ds((j // 2) * 8 + k * 2 + j % 2, 16, stride=16)
            near[k][j] = mid[rows, :] + pair[rows, :] + other[rows, :]


def sum_kernel(got, na, nb, nc, nd, efie, dual):
    marks = got[pl.ds(16, 64, stride=17), :].T
    pick = jnp.concatenate([marks[k * 16 : k * 16 + 16, :] for k in range(4)], axis=1).astype(BF16)
    pick = jnp.concatenate([pick, pick], axis=1)
    sums = []
    for j in range(4):
        value = jnp.concatenate([got[pl.ds(k * 4 + j, 64, stride=17), :] for k in range(4)], axis=0)
        high, low = halves(value)
        far = dot(pick, jnp.concatenate([high, low], axis=0))
        sums.append(far + na[j] + nb[j] + nc[j] + nd[j])
    efie[...] = jnp.stack([sums[0], sums[1]], axis=1).astype(BF16)
    dual[...] = jnp.stack([sums[2], sums[3]], axis=1).astype(BF16)


SMEM = pl.BlockSpec(memory_space=pltpu.SMEM)
VMEM = pl.BlockSpec(memory_space=pltpu.VMEM)
ANY = pl.BlockSpec(memory_space=pl.ANY)


def per_device(
    adjoint_input,
    efie_left,
    efie_right,
    dual_left,
    dual_right,
    block_ranks,
    far_cols,
    efie_near,
    dual_near,
    near_cols,
):
    per_dev = adjoint_input.shape[0]
    subs = lax.axis_size("sub")
    position = lax.axis_index("cluster")
    me = lax.axis_index("sub")
    me_ref = me.astype(jnp.int32).reshape(1)
    base = (position * per_dev - per_dev).astype(jnp.int32).reshape(1)
    x = adjoint_input.reshape(per_dev * 8, 128)
    params = pltpu.CompilerParams(vmem_limit_bytes=62 * MIB)
    small = pltpu.CompilerParams(vmem_limit_bytes=12 * MIB)

    def struct(shape, dtype=F32):
        return jax.ShapeDtypeStruct(shape, dtype)

    chunk = 4
    steps = per_dev // chunk
    far = pl.pallas_call(
        functools.partial(far_kernel, chunk),
        in_specs=[SMEM, SMEM, VMEM] + [ANY] * 4,
        out_specs=[ANY] * 4,
        out_shape=[struct((4, 128, 128))] * 4,
        scratch_shapes=[pltpu.VMEM(efie_left.shape, BF16)] * 4
        + [
            pltpu.VMEM((4, 4, 128, 128), F32),
            pltpu.VMEM((per_dev, 64, 256), BF16),
            pltpu.SemaphoreType.DMA((4, steps)),
            pltpu.SemaphoreType.DMA((4, steps)),
        ],
        compiler_params=params,
        cost_estimate=pl.CostEstimate(flops=200_000_000, bytes_accessed=5_300_000, transcendentals=0),
        name="far",
    )(me_ref, block_ranks.T, x, efie_left, efie_right, dual_left, dual_right)

    def shift(k):
        return [(i, (i + k) % subs) for i in range(subs)]

    far_got = [far[0]] + [lax.ppermute(far[k], "sub", shift(k)) for k in (1, 2, 3)]

    mid, pair, other = pl.pallas_call(
        functools.partial(near_kernel, chunk),
        in_specs=[SMEM, SMEM, SMEM, VMEM] + [ANY] * 3,
        out_specs=[VMEM] * 3,
        out_shape=[struct((per_dev, 2, 8, 128))] * 3,
        scratch_shapes=[pltpu.VMEM(efie_near.shape, BF16)] * 2
        + [pltpu.VMEM((3 * per_dev, 2, 8, 128), F32), pltpu.SemaphoreType.DMA((2, steps))],
        compiler_params=params,
        cost_estimate=pl.CostEstimate(flops=200_000_000, bytes_accessed=4_600_000, transcendentals=0),
        name="near",
    )(me_ref, base, near_cols.T, x, efie_near, dual_near, far[0])
    count = lax.axis_size("cluster")
    within = [(i, i ^ 1) for i in range(count)]
    between = [(i, i + 1) for i in range(1, count - 1, 2)] + [(i + 1, i) for i in range(1, count - 1, 2)]
    got_pair = lax.ppermute(pair, "cluster", within)
    got_other = lax.ppermute(other, "cluster", between)

    cols = far_cols.reshape(-1)
    owner = cols // per_dev
    earlier = (owner[:, None] == owner[None, :]) & (jnp.arange(128)[None, :] < jnp.arange(128)[:, None])
    order = jnp.sum(earlier.astype(jnp.int32), axis=1)
    slot = jnp.broadcast_to((owner * 4 + order)[None, :], (8, 128))
    place = jnp.broadcast_to((order * 16 + cols % per_dev)[:, None], (128, 128))
    sent, *near = pl.pallas_call(
        send_kernel,
        in_specs=[VMEM] * 9,
        out_specs=[VMEM] * 5,
        out_shape=[struct((count * 17, 128))] + [struct((4, per_dev, 128))] * 4,
        compiler_params=small,
        name="send",
    )(slot, place, *far_got, *(v.reshape(per_dev * 16, 128) for v in (mid, got_pair, got_other)))
    near_got = [near[0]] + [lax.ppermute(near[k], "sub", shift(k)) for k in (1, 2, 3)]
    got = lax.all_to_all(sent.reshape(count * 17, 1, 128), "cluster", 0, 0, tiled=True)
    efie, dual = pl.pallas_call(
        sum_kernel,
        in_specs=[VMEM] * 5,
        out_specs=[VMEM] * 2,
        out_shape=[struct((per_dev, 2, 128), BF16)] * 2,
        compiler_params=small,
        name="total",
    )(got.reshape(count * 17, 128), *near_got)
    shape = (per_dev, 2, 1, 128)
    return efie.reshape(shape), dual.reshape(shape)


def solution(mesh):
    return jax.shard_map(
        per_device,
        mesh=mesh,
        in_specs=(
            P("cluster", None, None, None),
            P("cluster", None, None, "sub", None),
            P("cluster", None, None, "sub", None),
            P("cluster", None, None, "sub", None),
            P("cluster", None, None, "sub", None),
            P("cluster", None),
            P("cluster", None),
            P("cluster", "sub", None, None, None),
            P("cluster", "sub", None, None, None),
            P("cluster", "sub"),
        ),
        out_specs=(P("cluster", None, "sub", None), P("cluster", None, "sub", None)),
        check_vma=False,
    )
```

```python
import functools

import jax
import jax.numpy as jnp
from jax import lax
from jax.experimental import pallas as pl
from jax.experimental.pallas import tpu as pltpu
from jax.sharding import PartitionSpec as P

F32 = jnp.float32
BF16 = jnp.bfloat16
MIB = 1024 * 1024


def iota(shape, dim):
    return lax.broadcasted_iota(jnp.int32, shape, dim)


def dot(left, right, dims=((1,), (0,))):
    return lax.dot_general(left, right, (dims, ((), ())), preferred_element_type=F32)


def vectors(x, me, cluster, copies):
    rows = 8 * copies
    shape = (2 * rows, x.shape[0])
    row, col = iota(shape, 0), iota(shape, 1)
    half = row // rows
    part = (row // copies) % 2
    vec = (me + (row % rows) // (2 * copies)) & 3
    wanted = cluster * 8 + jnp.where(half == part, 0, 1) * 4 + vec
    sign = jnp.where((half == 1) & (part == 1), -1.0, 1.0)
    both = dot(jnp.where(col == wanted, sign, 0.0).astype(BF16), x)
    return jnp.concatenate([both[:rows], both[rows:]], axis=1).astype(BF16)


def planes(ref, at, axis):
    return jnp.concatenate([ref[at, :, q].reshape(128, 128) for q in (0, 1)], axis=axis)


def far_kernel(chunk, me_ref, rank_ref, x_ref, le, re, ld, rd, o0, o1, o2, o3, ble, bre, bld, brd, made, lhs, sems, out_sems):
    outs = (o0, o1, o2, o3)
    clusters = ble.shape[0]
    steps = clusters // chunk

    def loads(i):
        part = pl.ds(i * chunk, chunk)
        pairs = ((le, ble), (ld, bld), (re, bre), (rd, brd))
        return [pltpu.make_async_copy(a.at[part], b.at[part], sems.at[j, i]) for j, (a, b) in enumerate(pairs)]

    def stores(i):
        part = pl.ds(i * chunk * 8, chunk * 8)
        return [pltpu.make_async_copy(made.at[k, :, part], outs[k].at[:, part], out_sems.at[k, i]) for k in (2, 1, 3, 0)]

    for i in range(steps):
        for copy in loads(i):
            copy.start()
    me = me_ref[0]
    x = x_ref[...]
    lane, sublane = iota((8, 128), 1), iota((8, 128), 0)
    for cluster in range(clusters):
        lhs[cluster] = vectors(x, me, cluster, 8)

    def spread(coef, keep):
        rows = [jnp.where(keep, coef[k * 8 : k * 8 + 8], 0.0) for k in range(8)]
        turned = [v for k in range(4) for v in (-rows[2 * k + 1], rows[2 * k])]
        both = [jnp.concatenate(rows, axis=0), jnp.concatenate(turned, axis=0)]
        return jnp.concatenate(both, axis=1).astype(BF16)

    def coefs(cluster):
        u = jnp.concatenate([planes(ble, cluster, 1), planes(bld, cluster, 1)], axis=0)
        return dot(lhs[cluster], u, ((1,), (1,)))

    def mixed(cluster, coef):
        ranks = jnp.zeros((8, 128), jnp.int32)
        for f in range(8):
            ranks = jnp.where(lane // 16 == f, rank_ref[f, cluster], ranks)
        keep = (lane // 16 == sublane) & (me * 16 + lane % 16 < ranks)
        return jnp.concatenate([spread(coef[:, :128], keep), spread(coef[:, 128:], keep)], axis=0)

    def results(cluster, mix):
        v = jnp.concatenate([planes(bre, cluster, 0), planes(brd, cluster, 0)], axis=1)
        far = dot(mix, v)
        for op in range(2):
            for k in range(4):
                for q in range(2):
                    start = op * 64 + k * 16 + q * 8
                    made[k, op * 2 + q, cluster * 8 : cluster * 8 + 8, :] = far[
                        start : start + 8, op * 128 : op * 128 + 128
                    ]

    for i in range(steps):
        copies = loads(i)
        these = range(i * chunk, i * chunk + chunk)
        for copy in copies[:2]:
            copy.wait()
        coef = [coefs(cluster) for cluster in these]
        mix = [mixed(cluster, c) for cluster, c in zip(these, coef)]
        for copy in copies[2:]:
            copy.wait()
        for cluster, m in zip(these, mix):
            results(cluster, m)
        for copy in stores(i):
            copy.start()
    for i in range(steps):
        for copy in stores(i):
            copy.wait()


def near_kernel(chunk, me_ref, base_ref, col_ref, x_ref, de, dd, after, mid, pair, other, bde, bdd, window, sems):
    clusters = bde.shape[0]
    steps = clusters // chunk

    def loads(i):
        part = pl.ds(i * chunk, chunk)
        pairs = ((de, bde), (dd, bdd))
        return [pltpu.make_async_copy(a.at[part], b.at[part], sems.at[j, i]) for j, (a, b) in enumerate(pairs)]

    for i in range(steps):
        for copy in loads(i):
            copy.start()
    me, base = me_ref[0], base_ref[0]
    x = x_ref[...]
    window[...] = jnp.zeros_like(window)
    lhs = [vectors(x, me, cluster, 1) for cluster in range(clusters)]
    for i in range(steps):
        for copy in loads(i):
            copy.wait()
        these = [(cluster, slot) for cluster in range(i * chunk, i * chunk + chunk) for slot in range(2)]
        outs = []
        for cluster, slot in these:
            d = jnp.concatenate([r[cluster, slot].reshape(256, 128) for r in (bde, bdd)], axis=1)
            outs.append(dot(lhs[cluster], d))
        for (cluster, slot), out in zip(these, outs):
            target = col_ref[slot, cluster] - base
            window[target, 0] += out[:, :128]
            window[target, 1] += out[:, 128:]
    odd = (base // 16) & 1 == 0
    mid[...] = window[16:32]
    pair[...] = window[pl.ds(jnp.where(odd, 0, 32), 16)]
    other[...] = window[pl.ds(jnp.where(odd, 32, 0), 16)]


def halves(value):
    high = value.astype(BF16)
    return high, (value - high.astype(F32)).astype(BF16)


def send_kernel(slot_ref, cols_ref, a, b, c, d, after, passed, out, passed_out):
    slot = jnp.broadcast_to(slot_ref[0:1, :], (64, 128))
    target = iota((64, 128), 0)
    picks = [jnp.where(slot == target * 4 + k, 1.0, 0.0).astype(BF16) for k in range(4)]
    pick = jnp.concatenate(picks, axis=0)
    pick = jnp.concatenate([pick, pick], axis=1)
    for half in range(2):
        parts = []
        for j in (half * 2, half * 2 + 1):
            high, low = halves(a[j] + b[j] + c[j] + d[j])
            parts.append(jnp.concatenate([high, low], axis=0))
        moved = dot(pick, jnp.concatenate(parts, axis=1))
        for q in range(2):
            for k in range(4):
                rows = pl.ds(k * 4 + half * 2 + q, 64, stride=17)
                out[rows, :] = moved[k * 64 : k * 64 + 64, q * 128 : q * 128 + 128]
    here = jnp.where(slot // 4 == target, 1.0, 0.0).astype(BF16)
    place = jnp.where(cols_ref[...] == iota((128, 128), 1), 1.0, 0.0).astype(BF16)
    out[pl.ds(16, 64, stride=17), :] = dot(here, place)


def merge_kernel(mid, pair, other, *near):
    for k in range(4):
        for j in range(4):
            rows = pl.ds((j // 2) * 8 + k * 2 + j % 2, 16, stride=16)
            near[k][j] = mid[rows, :] + pair[rows, :] + other[rows, :]


def sum_kernel(got, na, nb, nc, nd, efie, dual):
    marks = got[pl.ds(16, 64, stride=17), :].T
    pick = jnp.concatenate([marks[k * 16 : k * 16 + 16, :] for k in range(4)], axis=1).astype(BF16)
    pick = jnp.concatenate([pick, pick], axis=1)
    sums = []
    for j in range(4):
        value = jnp.concatenate([got[pl.ds(k * 4 + j, 64, stride=17), :] for k in range(4)], axis=0)
        high, low = halves(value)
        far = dot(pick, jnp.concatenate([high, low], axis=0))
        sums.append(far + na[j] + nb[j] + nc[j] + nd[j])
    efie[...] = jnp.stack([sums[0], sums[1]], axis=1).astype(BF16)
    dual[...] = jnp.stack([sums[2], sums[3]], axis=1).astype(BF16)


SMEM = pl.BlockSpec(memory_space=pltpu.SMEM)
VMEM = pl.BlockSpec(memory_space=pltpu.VMEM)
ANY = pl.BlockSpec(memory_space=pl.ANY)


def per_device(
    adjoint_input,
    efie_left,
    efie_right,
    dual_left,
    dual_right,
    block_ranks,
    far_cols,
    efie_near,
    dual_near,
    near_cols,
):
    per_dev = adjoint_input.shape[0]
    subs = lax.axis_size("sub")
    position = lax.axis_index("cluster")
    me = lax.axis_index("sub")
    me_ref = me.astype(jnp.int32).reshape(1)
    base = (position * per_dev - per_dev).astype(jnp.int32).reshape(1)
    x = adjoint_input.reshape(per_dev * 8, 128)
    params = pltpu.CompilerParams(vmem_limit_bytes=62 * MIB)
    small = pltpu.CompilerParams(vmem_limit_bytes=12 * MIB)

    def struct(shape, dtype=F32):
        return jax.ShapeDtypeStruct(shape, dtype)

    chunk = 4
    steps = per_dev // chunk
    far = pl.pallas_call(
        functools.partial(far_kernel, chunk),
        in_specs=[SMEM, SMEM, VMEM] + [ANY] * 4,
        out_specs=[ANY] * 4,
        out_shape=[struct((4, 128, 128))] * 4,
        scratch_shapes=[pltpu.VMEM(efie_left.shape, BF16)] * 4
        + [
            pltpu.VMEM((4, 4, 128, 128), F32),
            pltpu.VMEM((per_dev, 64, 256), BF16),
            pltpu.SemaphoreType.DMA((4, steps)),
            pltpu.SemaphoreType.DMA((4, steps)),
        ],
        compiler_params=params,
        cost_estimate=pl.CostEstimate(flops=200_000_000, bytes_accessed=5_300_000, transcendentals=0),
        name="far",
    )(me_ref, block_ranks.T, x, efie_left, efie_right, dual_left, dual_right)

    def shift(k):
        return [(i, (i + k) % subs) for i in range(subs)]

    def over_sub(parts):
        one, three, two = (lax.ppermute(parts[k], "sub", shift(k)) for k in (1, 3, 2))
        return [parts[0], one, two, three]

    far_got = over_sub(far)

    mid, pair, other = pl.pallas_call(
        functools.partial(near_kernel, chunk),
        in_specs=[SMEM, SMEM, SMEM, VMEM] + [ANY] * 3,
        out_specs=[VMEM] * 3,
        out_shape=[struct((per_dev, 2, 8, 128))] * 3,
        scratch_shapes=[pltpu.VMEM(efie_near.shape, BF16)] * 2
        + [pltpu.VMEM((3 * per_dev, 2, 8, 128), F32), pltpu.SemaphoreType.DMA((2, steps))],
        compiler_params=params,
        cost_estimate=pl.CostEstimate(flops=200_000_000, bytes_accessed=4_600_000, transcendentals=0),
        name="near",
    )(me_ref, base, near_cols.T, x, efie_near, dual_near, far[0])
    count = lax.axis_size("cluster")
    within = [(i, i ^ 1) for i in range(count)]
    between = [(i, i + 1) for i in range(1, count - 1, 2)] + [(i + 1, i) for i in range(1, count - 1, 2)]
    got_pair = lax.ppermute(pair, "cluster", within)
    got_other = lax.ppermute(other, "cluster", between)

    cols = far_cols.reshape(-1)
    owner = cols // per_dev
    earlier = (owner[:, None] == owner[None, :]) & (jnp.arange(128)[None, :] < jnp.arange(128)[:, None])
    order = jnp.sum(earlier.astype(jnp.int32), axis=1)
    slot = jnp.broadcast_to((owner * 4 + order)[None, :], (8, 128))
    place = jnp.broadcast_to((order * 16 + cols % per_dev)[:, None], (128, 128))
    sent, got_pair = pl.pallas_call(
        send_kernel,
        in_specs=[VMEM] * 6 + [ANY] * 2,
        out_specs=[VMEM, ANY],
        out_shape=[struct((count * 17, 128)), struct(pair.shape)],
        input_output_aliases={7: 1},
        compiler_params=small,
        name="send",
    )(slot, place, *far_got, got_other, got_pair)
    near = pl.pallas_call(
        merge_kernel,
        in_specs=[VMEM] * 3,
        out_specs=[VMEM] * 4,
        out_shape=[struct((4, per_dev, 128))] * 4,
        compiler_params=small,
        name="merge",
    )(*(v.reshape(per_dev * 16, 128) for v in (mid, got_pair, got_other)))
    near_got = over_sub(near)
    got = lax.all_to_all(sent.reshape(count * 17, 1, 128), "cluster", 0, 0, tiled=True)
    efie, dual = pl.pallas_call(
        sum_kernel,
        in_specs=[VMEM] * 5,
        out_specs=[VMEM] * 2,
        out_shape=[struct((per_dev, 2, 128), BF16)] * 2,
        compiler_params=small,
        name="total",
    )(got.reshape(count * 17, 128), *near_got)
    shape = (per_dev, 2, 1, 128)
    return efie.reshape(shape), dual.reshape(shape)


def solution(mesh):
    return jax.shard_map(
        per_device,
        mesh=mesh,
        in_specs=(
            P("cluster", None, None, None),
            P("cluster", None, None, "sub", None),
            P("cluster", None, None, "sub", None),
            P("cluster", None, None, "sub", None),
            P("cluster", None, None, "sub", None),
            P("cluster", None),
            P("cluster", None),
            P("cluster", "sub", None, None, None),
            P("cluster", "sub", None, None, None),
            P("cluster", "sub"),
        ),
        out_specs=(P("cluster", None, "sub", None), P("cluster", None, "sub", None)),
        check_vma=False,
    )
```

```python
import functools

import jax
import jax.numpy as jnp
from jax import lax
from jax.experimental import pallas as pl
from jax.experimental.pallas import tpu as pltpu
from jax.sharding import PartitionSpec as P

F32 = jnp.float32
BF16 = jnp.bfloat16
MIB = 1024 * 1024


def iota(shape, dim):
    return lax.broadcasted_iota(jnp.int32, shape, dim)


def dot(left, right, dims=((1,), (0,))):
    return lax.dot_general(left, right, (dims, ((), ())), preferred_element_type=F32)


def vectors(x, me, cluster, copies):
    rows = 8 * copies
    shape = (2 * rows, x.shape[0])
    row, col = iota(shape, 0), iota(shape, 1)
    half = row // rows
    part = (row // copies) % 2
    vec = (me + (row % rows) // (2 * copies)) & 3
    wanted = cluster * 8 + jnp.where(half == part, 0, 1) * 4 + vec
    sign = jnp.where((half == 1) & (part == 1), -1.0, 1.0)
    both = dot(jnp.where(col == wanted, sign, 0.0).astype(BF16), x)
    return jnp.concatenate([both[:rows], both[rows:]], axis=1).astype(BF16)


def planes(ref, at, axis):
    return jnp.concatenate([ref[at, :, q].reshape(128, 128) for q in (0, 1)], axis=axis)


def far_kernel(chunk, me_ref, rank_ref, x_ref, le, re, ld, rd, *rest):
    *outs, ble, bre, bld, brd, lhs, sems = rest
    clusters = ble.shape[0]
    steps = clusters // chunk

    def loads(i):
        part = pl.ds(i * chunk, chunk)
        pairs = ((le, ble), (ld, bld), (re, bre), (rd, brd))
        return [pltpu.make_async_copy(a.at[part], b.at[part], sems.at[j, i]) for j, (a, b) in enumerate(pairs)]

    for i in range(steps):
        for copy in loads(i):
            copy.start()
    me = me_ref[0]
    x = x_ref[...]
    lane, sublane = iota((8, 128), 1), iota((8, 128), 0)
    for cluster in range(clusters):
        lhs[cluster] = vectors(x, me, cluster, 8)

    def spread(coef, keep):
        rows = [jnp.where(keep, coef[k * 8 : k * 8 + 8], 0.0) for k in range(8)]
        turned = [v for k in range(4) for v in (-rows[2 * k + 1], rows[2 * k])]
        both = [jnp.concatenate(rows, axis=0), jnp.concatenate(turned, axis=0)]
        return jnp.concatenate(both, axis=1).astype(BF16)

    def coefs(cluster):
        u = jnp.concatenate([planes(ble, cluster, 1), planes(bld, cluster, 1)], axis=0)
        return dot(lhs[cluster], u, ((1,), (1,)))

    def mixed(cluster, coef):
        ranks = jnp.zeros((8, 128), jnp.int32)
        for f in range(8):
            ranks = jnp.where(lane // 16 == f, rank_ref[f, cluster], ranks)
        keep = (lane // 16 == sublane) & (me * 16 + lane % 16 < ranks)
        return jnp.concatenate([spread(coef[:, :128], keep), spread(coef[:, 128:], keep)], axis=0)

    def results(cluster, mix):
        v = jnp.concatenate([planes(bre, cluster, 0), planes(brd, cluster, 0)], axis=1)
        far = dot(mix, v)
        for op in range(2):
            for k in range(4):
                for q in range(2):
                    start = op * 64 + k * 16 + q * 8
                    outs[k][op * 2 + q, cluster * 8 : cluster * 8 + 8, :] = far[
                        start : start + 8, op * 128 : op * 128 + 128
                    ]

    for i in range(steps):
        copies = loads(i)
        these = range(i * chunk, i * chunk + chunk)
        for copy in copies[:2]:
            copy.wait()
        coef = [coefs(cluster) for cluster in these]
        mix = [mixed(cluster, c) for cluster, c in zip(these, coef)]
        for copy in copies[2:]:
            copy.wait()
        for cluster, m in zip(these, mix):
            results(cluster, m)

def near_kernel(chunk, me_ref, base_ref, col_ref, x_ref, de, dd, after, mid, pair, other, bde, bdd, window, sems):
    clusters = bde.shape[0]
    steps = clusters // chunk

    def loads(i):
        part = pl.ds(i * chunk, chunk)
        pairs = ((de, bde), (dd, bdd))
        return [pltpu.make_async_copy(a.at[part], b.at[part], sems.at[j, i]) for j, (a, b) in enumerate(pairs)]

    for i in range(steps):
        for copy in loads(i):
            copy.start()
    me, base = me_ref[0], base_ref[0]
    x = x_ref[...]
    window[...] = jnp.zeros_like(window)
    lhs = [vectors(x, me, cluster, 1) for cluster in range(clusters)]
    for i in range(steps):
        for copy in loads(i):
            copy.wait()
        these = [(cluster, slot) for cluster in range(i * chunk, i * chunk + chunk) for slot in range(2)]
        outs = []
        for cluster, slot in these:
            d = jnp.concatenate([r[cluster, slot].reshape(256, 128) for r in (bde, bdd)], axis=1)
            outs.append(dot(lhs[cluster], d))
        for (cluster, slot), out in zip(these, outs):
            target = col_ref[slot, cluster] - base
            window[target, 0] += out[:, :128]
            window[target, 1] += out[:, 128:]
    odd = (base // 16) & 1 == 0
    mid[...] = window[16:32]
    pair[...] = window[pl.ds(jnp.where(odd, 0, 32), 16)]
    other[...] = window[pl.ds(jnp.where(odd, 32, 0), 16)]


def halves(value):
    high = value.astype(BF16)
    return high, (value - high.astype(F32)).astype(BF16)


def send_kernel(slot_ref, cols_ref, a, b, c, d, out):
    slot = jnp.broadcast_to(slot_ref[0:1, :], (64, 128))
    target = iota((64, 128), 0)
    picks = [jnp.where(slot == target * 4 + k, 1.0, 0.0).astype(BF16) for k in range(4)]
    pick = jnp.concatenate(picks, axis=0)
    pick = jnp.concatenate([pick, pick], axis=1)
    for half in range(2):
        parts = []
        for j in (half * 2, half * 2 + 1):
            high, low = halves(a[j] + b[j] + c[j] + d[j])
            parts.append(jnp.concatenate([high, low], axis=0))
        moved = dot(pick, jnp.concatenate(parts, axis=1))
        for q in range(2):
            for k in range(4):
                rows = pl.ds(k * 4 + half * 2 + q, 64, stride=17)
                out[rows, :] = moved[k * 64 : k * 64 + 64, q * 128 : q * 128 + 128]
    here = jnp.where(slot // 4 == target, 1.0, 0.0).astype(BF16)
    place = jnp.where(cols_ref[...] == iota((128, 128), 1), 1.0, 0.0).astype(BF16)
    out[pl.ds(16, 64, stride=17), :] = dot(here, place)


def merge_kernel(mid, pair, other, *near):
    for k in range(4):
        for j in range(4):
            rows = pl.ds((j // 2) * 8 + k * 2 + j % 2, 16, stride=16)
            near[k][j] = mid[rows, :] + pair[rows, :] + other[rows, :]


def sum_kernel(got, na, nb, nc, nd, efie, dual):
    marks = got[pl.ds(16, 64, stride=17), :].T
    pick = jnp.concatenate([marks[k * 16 : k * 16 + 16, :] for k in range(4)], axis=1).astype(BF16)
    pick = jnp.concatenate([pick, pick], axis=1)
    sums = []
    for j in range(4):
        value = jnp.concatenate([got[pl.ds(k * 4 + j, 64, stride=17), :] for k in range(4)], axis=0)
        high, low = halves(value)
        far = dot(pick, jnp.concatenate([high, low], axis=0))
        sums.append(far + na[j] + nb[j] + nc[j] + nd[j])
    efie[...] = jnp.stack([sums[0], sums[1]], axis=1).astype(BF16)
    dual[...] = jnp.stack([sums[2], sums[3]], axis=1).astype(BF16)


SMEM = pl.BlockSpec(memory_space=pltpu.SMEM)
VMEM = pl.BlockSpec(memory_space=pltpu.VMEM)
ANY = pl.BlockSpec(memory_space=pl.ANY)


def per_device(
    adjoint_input,
    efie_left,
    efie_right,
    dual_left,
    dual_right,
    block_ranks,
    far_cols,
    efie_near,
    dual_near,
    near_cols,
):
    per_dev = adjoint_input.shape[0]
    subs = lax.axis_size("sub")
    position = lax.axis_index("cluster")
    me = lax.axis_index("sub")
    me_ref = me.astype(jnp.int32).reshape(1)
    base = (position * per_dev - per_dev).astype(jnp.int32).reshape(1)
    x = adjoint_input.reshape(per_dev * 8, 128)
    params = pltpu.CompilerParams(vmem_limit_bytes=24 * MIB)
    small = pltpu.CompilerParams(vmem_limit_bytes=12 * MIB)

    def struct(shape, dtype=F32):
        return jax.ShapeDtypeStruct(shape, dtype)

    def in_hbm(*values):
        return [pltpu.with_memory_space_constraint(v, pltpu.HBM) for v in values]

    chunk = 4
    steps = per_dev // chunk
    far = pl.pallas_call(
        functools.partial(far_kernel, chunk),
        in_specs=[SMEM, SMEM, VMEM] + [ANY] * 4,
        out_specs=[VMEM] * 4,
        out_shape=[struct((4, 128, 128), F32)] * 4,
        scratch_shapes=[pltpu.VMEM(efie_left.shape, BF16)] * 4
        + [pltpu.VMEM((per_dev, 64, 256), BF16), pltpu.SemaphoreType.DMA((4, steps))],
        compiler_params=params,
        cost_estimate=pl.CostEstimate(flops=200_000_000, bytes_accessed=5_300_000, transcendentals=0),
        name="far",
    )(me_ref, *in_hbm(block_ranks.T, x, efie_left, efie_right, dual_left, dual_right))

    def shift(k):
        return [(i, (i + k) % subs) for i in range(subs)]

    def over_sub(parts):
        one, three, two = (lax.ppermute(parts[k], "sub", shift(k)) for k in (1, 3, 2))
        return [parts[0], one, two, three]

    far_got = over_sub(far)

    mid, pair, other = pl.pallas_call(
        functools.partial(near_kernel, chunk),
        in_specs=[SMEM, SMEM, SMEM, VMEM] + [ANY] * 3,
        out_specs=[VMEM] * 3,
        out_shape=[struct((per_dev, 2, 8, 128))] * 3,
        scratch_shapes=[pltpu.VMEM(efie_near.shape, BF16)] * 2
        + [pltpu.VMEM((3 * per_dev, 2, 8, 128), F32), pltpu.SemaphoreType.DMA((2, steps))],
        compiler_params=params,
        cost_estimate=pl.CostEstimate(flops=200_000_000, bytes_accessed=4_600_000, transcendentals=0),
        name="near",
    )(me_ref, base, *in_hbm(near_cols.T, x, efie_near, dual_near), far[0])
    count = lax.axis_size("cluster")
    within = [(i, i ^ 1) for i in range(count)]
    between = [(i, i + 1) for i in range(1, count - 1, 2)] + [(i + 1, i) for i in range(1, count - 1, 2)]
    got_pair = lax.ppermute(pair, "cluster", within)
    got_other = lax.ppermute(other, "cluster", between)

    cols = far_cols.reshape(-1)
    owner = cols // per_dev
    earlier = (owner[:, None] == owner[None, :]) & (jnp.arange(128)[None, :] < jnp.arange(128)[:, None])
    order = jnp.sum(earlier.astype(jnp.int32), axis=1)
    slot = jnp.broadcast_to((owner * 4 + order)[None, :], (8, 128))
    place = jnp.broadcast_to((order * 16 + cols % per_dev)[:, None], (128, 128))
    sent = pl.pallas_call(
        send_kernel,
        in_specs=[VMEM] * 6,
        out_specs=VMEM,
        out_shape=struct((count * 17, 128)),
        compiler_params=small,
        name="send",
    )(slot, place, *far_got)
    sent, got_pair, got_other = pl.pallas_call(
        lambda *refs: None,
        in_specs=[ANY] * 3,
        out_specs=[ANY] * 3,
        out_shape=[struct((count * 17, 128)), struct(pair.shape), struct(pair.shape)],
        input_output_aliases={0: 0, 1: 1, 2: 2},
        compiler_params=small,
        name="join",
    )(sent, got_pair, got_other)
    near = pl.pallas_call(
        merge_kernel,
        in_specs=[VMEM] * 3,
        out_specs=[VMEM] * 4,
        out_shape=[struct((4, per_dev, 128))] * 4,
        compiler_params=small,
        name="merge",
    )(*(v.reshape(per_dev * 16, 128) for v in (mid, got_pair, got_other)))
    near_got = over_sub(near)
    got = lax.all_to_all(sent.reshape(count * 17, 1, 128), "cluster", 0, 0, tiled=True)
    efie, dual = pl.pallas_call(
        sum_kernel,
        in_specs=[VMEM] * 5,
        out_specs=[VMEM] * 2,
        out_shape=[struct((per_dev, 2, 128), BF16)] * 2,
        compiler_params=small,
        name="total",
    )(got.reshape(count * 17, 128), *near_got)
    shape = (per_dev, 2, 1, 128)
    return efie.reshape(shape), dual.reshape(shape)


def solution(mesh):
    return jax.shard_map(
        per_device,
        mesh=mesh,
        in_specs=(
            P("cluster", None, None, None),
            P("cluster", None, None, "sub", None),
            P("cluster", None, None, "sub", None),
            P("cluster", None, None, "sub", None),
            P("cluster", None, None, "sub", None),
            P("cluster", None),
            P("cluster", None),
            P("cluster", "sub", None, None, None),
            P("cluster", "sub", None, None, None),
            P("cluster", "sub"),
        ),
        out_specs=(P("cluster", None, "sub", None), P("cluster", None, "sub", None)),
        check_vma=False,
    )
```

```python
import functools

import jax
import jax.numpy as jnp
from jax import lax
from jax.experimental import pallas as pl
from jax.experimental.pallas import tpu as pltpu
from jax.sharding import PartitionSpec as P

F32 = jnp.float32
BF16 = jnp.bfloat16
MIB = 1024 * 1024


def iota(shape, dim):
    return lax.broadcasted_iota(jnp.int32, shape, dim)


def dot(left, right, dims=((1,), (0,))):
    return lax.dot_general(left, right, (dims, ((), ())), preferred_element_type=F32)


def vectors(x, me, cluster, copies):
    rows = 8 * copies
    shape = (2 * rows, x.shape[0])
    row, col = iota(shape, 0), iota(shape, 1)
    half = row // rows
    part = (row // copies) % 2
    vec = (me + (row % rows) // (2 * copies)) & 3
    wanted = cluster * 8 + jnp.where(half == part, 0, 1) * 4 + vec
    sign = jnp.where((half == 1) & (part == 1), -1.0, 1.0)
    both = dot(jnp.where(col == wanted, sign, 0.0).astype(BF16), x)
    return jnp.concatenate([both[:rows], both[rows:]], axis=1).astype(BF16)


def planes(ref, at, axis):
    return jnp.concatenate([ref[at, :, q].reshape(128, 128) for q in (0, 1)], axis=axis)


def far_kernel(chunk, me_ref, rank_ref, x_ref, le, re, ld, rd, *rest):
    *outs, ble, bre, bld, brd, lhs, sems = rest
    clusters = ble.shape[0]
    steps = clusters // chunk

    def loads(i):
        part = pl.ds(i * chunk, chunk)
        pairs = ((le, ble), (ld, bld), (re, bre), (rd, brd))
        return [pltpu.make_async_copy(a.at[part], b.at[part], sems.at[j, i]) for j, (a, b) in enumerate(pairs)]

    for i in range(steps):
        for copy in loads(i):
            copy.start()
    me = me_ref[0]
    x = x_ref[...]
    lane, sublane = iota((8, 128), 1), iota((8, 128), 0)
    for cluster in range(clusters):
        lhs[cluster] = vectors(x, me, cluster, 8)

    def spread(coef, keep):
        rows = [jnp.where(keep, coef[k * 8 : k * 8 + 8], 0.0) for k in range(8)]
        turned = [v for k in range(4) for v in (-rows[2 * k + 1], rows[2 * k])]
        both = [jnp.concatenate(rows, axis=0), jnp.concatenate(turned, axis=0)]
        return jnp.concatenate(both, axis=1).astype(BF16)

    def coefs(cluster):
        u = jnp.concatenate([planes(ble, cluster, 1), planes(bld, cluster, 1)], axis=0)
        return dot(lhs[cluster], u, ((1,), (1,)))

    def mixed(cluster, coef):
        ranks = jnp.zeros((8, 128), jnp.int32)
        for f in range(8):
            ranks = jnp.where(lane // 16 == f, rank_ref[f, cluster], ranks)
        keep = (lane // 16 == sublane) & (me * 16 + lane % 16 < ranks)
        return jnp.concatenate([spread(coef[:, :128], keep), spread(coef[:, 128:], keep)], axis=0)

    def results(cluster, mix):
        v = jnp.concatenate([planes(bre, cluster, 0), planes(brd, cluster, 0)], axis=1)
        far = dot(mix, v)
        for op in range(2):
            for k in range(4):
                for q in range(2):
                    start = op * 64 + k * 16 + q * 8
                    outs[k][op * 2 + q, cluster * 8 : cluster * 8 + 8, :] = far[
                        start : start + 8, op * 128 : op * 128 + 128
                    ]

    for i in range(steps):
        copies = loads(i)
        these = range(i * chunk, i * chunk + chunk)
        for copy in copies[:2]:
            copy.wait()
        coef = [coefs(cluster) for cluster in these]
        mix = [mixed(cluster, c) for cluster, c in zip(these, coef)]
        for copy in copies[2:]:
            copy.wait()
        for cluster, m in zip(these, mix):
            results(cluster, m)

def near_kernel(chunk, me_ref, base_ref, col_ref, x_ref, de, dd, after, mid, pair, other, bde, bdd, window, sems):
    clusters = bde.shape[0]
    steps = clusters // chunk

    def loads(i):
        part = pl.ds(i * chunk, chunk)
        pairs = ((de, bde), (dd, bdd))
        return [pltpu.make_async_copy(a.at[part], b.at[part], sems.at[j, i]) for j, (a, b) in enumerate(pairs)]

    for i in range(steps):
        for copy in loads(i):
            copy.start()
    me, base = me_ref[0], base_ref[0]
    x = x_ref[...]
    window[...] = jnp.zeros_like(window)
    lhs = [vectors(x, me, cluster, 1) for cluster in range(clusters)]
    for i in range(steps):
        for copy in loads(i):
            copy.wait()
        these = [(cluster, slot) for cluster in range(i * chunk, i * chunk + chunk) for slot in range(2)]
        outs = []
        for cluster, slot in these:
            d = jnp.concatenate([r[cluster, slot].reshape(256, 128) for r in (bde, bdd)], axis=1)
            outs.append(dot(lhs[cluster], d))
        for (cluster, slot), out in zip(these, outs):
            target = col_ref[slot, cluster] - base
            window[target, 0] += out[:, :128]
            window[target, 1] += out[:, 128:]
    odd = (base // 16) & 1 == 0
    mid[...] = window[16:32]
    pair[...] = window[pl.ds(jnp.where(odd, 0, 32), 16)]
    other[...] = window[pl.ds(jnp.where(odd, 32, 0), 16)]


def halves(value):
    high = value.astype(BF16)
    return high, (value - high.astype(F32)).astype(BF16)


def send_kernel(slot_ref, cols_ref, a, b, c, d, out):
    slot = jnp.broadcast_to(slot_ref[0:1, :], (64, 128))
    target = iota((64, 128), 0)
    picks = [jnp.where(slot == target * 4 + k, 1.0, 0.0).astype(BF16) for k in range(4)]
    pick = jnp.concatenate(picks, axis=0)
    pick = jnp.concatenate([pick, pick], axis=1)
    for half in range(2):
        parts = []
        for j in (half * 2, half * 2 + 1):
            high, low = halves(a[j] + b[j] + c[j] + d[j])
            parts.append(jnp.concatenate([high, low], axis=0))
        moved = dot(pick, jnp.concatenate(parts, axis=1))
        for q in range(2):
            for k in range(4):
                rows = pl.ds(k * 4 + half * 2 + q, 64, stride=17)
                out[rows, :] = moved[k * 64 : k * 64 + 64, q * 128 : q * 128 + 128]
    here = jnp.where(slot // 4 == target, 1.0, 0.0).astype(BF16)
    place = jnp.where(cols_ref[...] == iota((128, 128), 1), 1.0, 0.0).astype(BF16)
    out[pl.ds(16, 64, stride=17), :] = dot(here, place)


def merge_kernel(mid, pair, other, *near):
    for k in range(4):
        for j in range(4):
            rows = pl.ds((j // 2) * 8 + k * 2 + j % 2, 16, stride=16)
            near[k][j] = mid[rows, :] + pair[rows, :] + other[rows, :]


def sum_kernel(got, na, nb, nc, nd, efie, dual):
    marks = got[pl.ds(16, 64, stride=17), :].T
    pick = jnp.concatenate([marks[k * 16 : k * 16 + 16, :] for k in range(4)], axis=1).astype(BF16)
    pick = jnp.concatenate([pick, pick], axis=1)
    sums = []
    for j in range(4):
        value = jnp.concatenate([got[pl.ds(k * 4 + j, 64, stride=17), :] for k in range(4)], axis=0)
        high, low = halves(value)
        far = dot(pick, jnp.concatenate([high, low], axis=0))
        sums.append(far + na[j] + nb[j] + nc[j] + nd[j])
    efie[...] = jnp.stack([sums[0], sums[1]], axis=1).astype(BF16)
    dual[...] = jnp.stack([sums[2], sums[3]], axis=1).astype(BF16)


SMEM = pl.BlockSpec(memory_space=pltpu.SMEM)
VMEM = pl.BlockSpec(memory_space=pltpu.VMEM)
ANY = pl.BlockSpec(memory_space=pl.ANY)


def per_device(
    adjoint_input,
    efie_left,
    efie_right,
    dual_left,
    dual_right,
    block_ranks,
    far_cols,
    efie_near,
    dual_near,
    near_cols,
):
    per_dev = adjoint_input.shape[0]
    subs = lax.axis_size("sub")
    position = lax.axis_index("cluster")
    me = lax.axis_index("sub")
    me_ref = me.astype(jnp.int32).reshape(1)
    base = (position * per_dev - per_dev).astype(jnp.int32).reshape(1)
    x = adjoint_input.reshape(per_dev * 8, 128)
    params = pltpu.CompilerParams(vmem_limit_bytes=24 * MIB)
    small = pltpu.CompilerParams(vmem_limit_bytes=12 * MIB)

    def struct(shape, dtype=F32):
        return jax.ShapeDtypeStruct(shape, dtype)

    def in_hbm(*values):
        return [pltpu.with_memory_space_constraint(v, pltpu.HBM) for v in values]

    chunk = 8
    steps = per_dev // chunk
    far = pl.pallas_call(
        functools.partial(far_kernel, chunk),
        in_specs=[SMEM, SMEM, VMEM] + [ANY] * 4,
        out_specs=[VMEM] * 4,
        out_shape=[struct((4, 128, 128), F32)] * 4,
        scratch_shapes=[pltpu.VMEM(efie_left.shape, BF16)] * 4
        + [pltpu.VMEM((per_dev, 64, 256), BF16), pltpu.SemaphoreType.DMA((4, steps))],
        compiler_params=params,
        cost_estimate=pl.CostEstimate(flops=200_000_000, bytes_accessed=5_300_000, transcendentals=0),
        name="far",
    )(me_ref, *in_hbm(block_ranks.T, x, efie_left, efie_right, dual_left, dual_right))

    def shift(k):
        return [(i, (i + k) % subs) for i in range(subs)]

    def over_sub(parts):
        return [parts[0]] + [lax.ppermute(parts[k], "sub", shift(k)) for k in (1, 3, 2)]

    far_got = over_sub(far)

    mid, pair, other = pl.pallas_call(
        functools.partial(near_kernel, chunk),
        in_specs=[SMEM, SMEM, SMEM, VMEM] + [ANY] * 3,
        out_specs=[VMEM] * 3,
        out_shape=[struct((per_dev, 2, 8, 128))] * 3,
        scratch_shapes=[pltpu.VMEM(efie_near.shape, BF16)] * 2
        + [pltpu.VMEM((3 * per_dev, 2, 8, 128), F32), pltpu.SemaphoreType.DMA((2, steps))],
        compiler_params=params,
        cost_estimate=pl.CostEstimate(flops=200_000_000, bytes_accessed=4_600_000, transcendentals=0),
        name="near",
    )(me_ref, base, *in_hbm(near_cols.T, x, efie_near, dual_near), far[0])
    count = lax.axis_size("cluster")
    within = [(i, i ^ 1) for i in range(count)]
    between = [(i, i + 1) for i in range(1, count - 1, 2)] + [(i + 1, i) for i in range(1, count - 1, 2)]
    got_pair = lax.ppermute(pair, "cluster", within)
    got_other = lax.ppermute(other, "cluster", between)

    cols = far_cols.reshape(-1)
    owner = cols // per_dev
    earlier = (owner[:, None] == owner[None, :]) & (jnp.arange(128)[None, :] < jnp.arange(128)[:, None])
    order = jnp.sum(earlier.astype(jnp.int32), axis=1)
    slot = jnp.broadcast_to((owner * 4 + order)[None, :], (8, 128))
    place = jnp.broadcast_to((order * 16 + cols % per_dev)[:, None], (128, 128))
    sent = pl.pallas_call(
        send_kernel,
        in_specs=[VMEM] * 6,
        out_specs=VMEM,
        out_shape=struct((count * 17, 128)),
        compiler_params=small,
        name="send",
    )(slot, place, *far_got)
    sent, got_pair, got_other = pl.pallas_call(
        lambda *refs: None,
        in_specs=[ANY] * 3,
        out_specs=[ANY] * 3,
        out_shape=[struct((count * 17, 128)), struct(pair.shape), struct(pair.shape)],
        input_output_aliases={0: 0, 1: 1, 2: 2},
        compiler_params=small,
        name="join",
    )(sent, got_pair, got_other)
    near = pl.pallas_call(
        merge_kernel,
        in_specs=[VMEM] * 3,
        out_specs=[VMEM] * 4,
        out_shape=[struct((4, per_dev, 128))] * 4,
        compiler_params=small,
        name="merge",
    )(*(v.reshape(per_dev * 16, 128) for v in (mid, got_pair, got_other)))
    near_got = over_sub(near)
    got = lax.all_to_all(sent.reshape(count * 17, 1, 128), "cluster", 0, 0, tiled=True)
    efie, dual = pl.pallas_call(
        sum_kernel,
        in_specs=[VMEM] * 5,
        out_specs=[VMEM] * 2,
        out_shape=[struct((per_dev, 2, 128), BF16)] * 2,
        compiler_params=small,
        name="total",
    )(got.reshape(count * 17, 128), *near_got)
    shape = (per_dev, 2, 1, 128)
    return efie.reshape(shape), dual.reshape(shape)


def solution(mesh):
    return jax.shard_map(
        per_device,
        mesh=mesh,
        in_specs=(
            P("cluster", None, None, None),
            P("cluster", None, None, "sub", None),
            P("cluster", None, None, "sub", None),
            P("cluster", None, None, "sub", None),
            P("cluster", None, None, "sub", None),
            P("cluster", None),
            P("cluster", None),
            P("cluster", "sub", None, None, None),
            P("cluster", "sub", None, None, None),
            P("cluster", "sub"),
        ),
        out_specs=(P("cluster", None, "sub", None), P("cluster", None, "sub", None)),
        check_vma=False,
    )
```

```python
import functools

import jax
import jax.numpy as jnp
from jax import lax
from jax.experimental import pallas as pl
from jax.experimental.pallas import tpu as pltpu
from jax.sharding import PartitionSpec as P

F32 = jnp.float32
BF16 = jnp.bfloat16
MIB = 1024 * 1024


def iota(shape, dim):
    return lax.broadcasted_iota(jnp.int32, shape, dim)


def dot(left, right, dims=((1,), (0,))):
    return lax.dot_general(left, right, (dims, ((), ())), preferred_element_type=F32)


def vectors(x, me, cluster, copies):
    rows = 8 * copies
    shape = (2 * rows, x.shape[0])
    row, col = iota(shape, 0), iota(shape, 1)
    half = row // rows
    part = (row // copies) % 2
    vec = (me + (row % rows) // (2 * copies)) & 3
    wanted = cluster * 8 + jnp.where(half == part, 0, 1) * 4 + vec
    sign = jnp.where((half == 1) & (part == 1), -1.0, 1.0)
    both = dot(jnp.where(col == wanted, sign, 0.0).astype(BF16), x)
    return jnp.concatenate([both[:rows], both[rows:]], axis=1).astype(BF16)


def planes(ref, at, axis):
    return jnp.concatenate([ref[at, :, q].reshape(128, 128) for q in (0, 1)], axis=axis)


def far_kernel(chunk, me_ref, rank_ref, x_ref, le, re, ld, rd, *rest):
    *outs, ble, bre, bld, brd, lhs, sems = rest
    clusters = ble.shape[0]
    steps = clusters // chunk

    def loads(i):
        part = pl.ds(i * chunk, chunk)
        pairs = ((le, ble), (ld, bld), (re, bre), (rd, brd))
        return [pltpu.make_async_copy(a.at[part], b.at[part], sems.at[j, i]) for j, (a, b) in enumerate(pairs)]

    for i in range(steps):
        for copy in loads(i):
            copy.start()
    me = me_ref[0]
    x = x_ref[...]
    lane, sublane = iota((8, 128), 1), iota((8, 128), 0)
    for cluster in range(clusters):
        lhs[cluster] = vectors(x, me, cluster, 8)

    def spread(coef, keep):
        rows = [jnp.where(keep, coef[k * 8 : k * 8 + 8], 0.0) for k in range(8)]
        turned = [v for k in range(4) for v in (-rows[2 * k + 1], rows[2 * k])]
        both = [jnp.concatenate(rows, axis=0), jnp.concatenate(turned, axis=0)]
        return jnp.concatenate(both, axis=1).astype(BF16)

    def coefs(cluster):
        u = jnp.concatenate([planes(ble, cluster, 1), planes(bld, cluster, 1)], axis=0)
        return dot(lhs[cluster], u, ((1,), (1,)))

    def mixed(cluster, coef):
        ranks = jnp.zeros((8, 128), jnp.int32)
        for f in range(8):
            ranks = jnp.where(lane // 16 == f, rank_ref[f, cluster], ranks)
        keep = (lane // 16 == sublane) & (me * 16 + lane % 16 < ranks)
        return jnp.concatenate([spread(coef[:, :128], keep), spread(coef[:, 128:], keep)], axis=0)

    def results(cluster, mix):
        v = jnp.concatenate([planes(bre, cluster, 0), planes(brd, cluster, 0)], axis=1)
        far = dot(mix, v)
        for op in range(2):
            for k in range(4):
                for q in range(2):
                    start = op * 64 + k * 16 + q * 8
                    outs[k][op * 2 + q, cluster * 8 : cluster * 8 + 8, :] = far[
                        start : start + 8, op * 128 : op * 128 + 128
                    ]

    for i in range(steps):
        copies = loads(i)
        these = range(i * chunk, i * chunk + chunk)
        for copy in copies[:2]:
            copy.wait()
        coef = [coefs(cluster) for cluster in these]
        mix = [mixed(cluster, c) for cluster, c in zip(these, coef)]
        for copy in copies[2:]:
            copy.wait()
        for cluster, m in zip(these, mix):
            results(cluster, m)

def near_kernel(chunk, me_ref, base_ref, col_ref, x_ref, de, dd, after, mid, pair, other, bde, bdd, window, sems):
    clusters = bde.shape[0]
    steps = clusters // chunk

    def loads(i):
        part = pl.ds(i * chunk, chunk)
        pairs = ((de, bde), (dd, bdd))
        return [pltpu.make_async_copy(a.at[part], b.at[part], sems.at[j, i]) for j, (a, b) in enumerate(pairs)]

    for i in range(steps):
        for copy in loads(i):
            copy.start()
    me, base = me_ref[0], base_ref[0]
    x = x_ref[...]
    window[...] = jnp.zeros_like(window)
    lhs = [vectors(x, me, cluster, 1) for cluster in range(clusters)]
    for i in range(steps):
        for copy in loads(i):
            copy.wait()
        these = [(cluster, slot) for cluster in range(i * chunk, i * chunk + chunk) for slot in range(2)]
        outs = []
        for cluster, slot in these:
            d = jnp.concatenate([r[cluster, slot].reshape(256, 128) for r in (bde, bdd)], axis=1)
            outs.append(dot(lhs[cluster], d))
        for (cluster, slot), out in zip(these, outs):
            target = col_ref[slot, cluster] - base
            window[target, 0] += out[:, :128]
            window[target, 1] += out[:, 128:]
    odd = (base // 16) & 1 == 0
    mid[...] = window[16:32]
    pair[...] = window[pl.ds(jnp.where(odd, 0, 32), 16)]
    other[...] = window[pl.ds(jnp.where(odd, 32, 0), 16)]


def halves(value):
    high = value.astype(BF16)
    return high, (value - high.astype(F32)).astype(BF16)


def send_kernel(slot_ref, cols_ref, a, b, c, d, out):
    slot = jnp.broadcast_to(slot_ref[0:1, :], (64, 128))
    target = iota((64, 128), 0)
    picks = [jnp.where(slot == target * 4 + k, 1.0, 0.0).astype(BF16) for k in range(4)]
    pick = jnp.concatenate(picks, axis=0)
    pick = jnp.concatenate([pick, pick], axis=1)
    for half in range(2):
        parts = []
        for j in (half * 2, half * 2 + 1):
            high, low = halves(a[j] + b[j] + c[j] + d[j])
            parts.append(jnp.concatenate([high, low], axis=0))
        moved = dot(pick, jnp.concatenate(parts, axis=1))
        for q in range(2):
            for k in range(4):
                rows = pl.ds(k * 4 + half * 2 + q, 64, stride=17)
                out[rows, :] = moved[k * 64 : k * 64 + 64, q * 128 : q * 128 + 128]
    here = jnp.where(slot // 4 == target, 1.0, 0.0).astype(BF16)
    place = jnp.where(cols_ref[...] == iota((128, 128), 1), 1.0, 0.0).astype(BF16)
    out[pl.ds(16, 64, stride=17), :] = dot(here, place)


def merge_kernel(mid, pair, other, *near):
    for k in range(4):
        for j in range(4):
            rows = pl.ds((j // 2) * 8 + k * 2 + j % 2, 16, stride=16)
            near[k][j] = mid[rows, :] + pair[rows, :] + other[rows, :]


def sum_kernel(got, na, nb, nc, nd, efie, dual):
    marks = got[pl.ds(16, 64, stride=17), :].T
    pick = jnp.concatenate([marks[k * 16 : k * 16 + 16, :] for k in range(4)], axis=1).astype(BF16)
    pick = jnp.concatenate([pick, pick], axis=1)
    sums = []
    for j in range(4):
        value = jnp.concatenate([got[pl.ds(k * 4 + j, 64, stride=17), :] for k in range(4)], axis=0)
        high, low = halves(value)
        far = dot(pick, jnp.concatenate([high, low], axis=0))
        sums.append(far + na[j] + nb[j] + nc[j] + nd[j])
    efie[...] = jnp.stack([sums[0], sums[1]], axis=1).astype(BF16)
    dual[...] = jnp.stack([sums[2], sums[3]], axis=1).astype(BF16)


def turn(index):
    z, y, core = index // 8, (index // 2) % 4, index % 2
    return z * 8 + (y + (z % 2) * (3 - 2 * y)) * 2 + (core + (y % 2) * (1 - 2 * core))


SMEM = pl.BlockSpec(memory_space=pltpu.SMEM)
VMEM = pl.BlockSpec(memory_space=pltpu.VMEM)
ANY = pl.BlockSpec(memory_space=pl.ANY)


def per_device(
    adjoint_input,
    efie_left,
    efie_right,
    dual_left,
    dual_right,
    block_ranks,
    far_cols,
    efie_near,
    dual_near,
    near_cols,
):
    per_dev = adjoint_input.shape[0]
    subs = lax.axis_size("sub")
    position = lax.axis_index("cluster")
    me = lax.axis_index("sub")
    me_ref = me.astype(jnp.int32).reshape(1)
    base = (position * per_dev - per_dev).astype(jnp.int32).reshape(1)
    x = adjoint_input.reshape(per_dev * 8, 128)
    params = pltpu.CompilerParams(vmem_limit_bytes=24 * MIB)
    small = pltpu.CompilerParams(vmem_limit_bytes=12 * MIB)

    def struct(shape, dtype=F32):
        return jax.ShapeDtypeStruct(shape, dtype)

    def in_hbm(*values):
        return [pltpu.with_memory_space_constraint(v, pltpu.HBM) for v in values]

    chunk = 8
    steps = per_dev // chunk
    far = pl.pallas_call(
        functools.partial(far_kernel, chunk),
        in_specs=[SMEM, SMEM, VMEM] + [ANY] * 4,
        out_specs=[VMEM] * 4,
        out_shape=[struct((4, 128, 128), F32)] * 4,
        scratch_shapes=[pltpu.VMEM(efie_left.shape, BF16)] * 4
        + [pltpu.VMEM((per_dev, 64, 256), BF16), pltpu.SemaphoreType.DMA((4, steps))],
        compiler_params=params,
        cost_estimate=pl.CostEstimate(flops=200_000_000, bytes_accessed=5_300_000, transcendentals=0),
        name="far",
    )(me_ref, *in_hbm(block_ranks.T, x, efie_left, efie_right, dual_left, dual_right))

    def shift(k):
        return [(i, (i + k) % subs) for i in range(subs)]

    def over_sub(parts):
        return [parts[0]] + [lax.ppermute(parts[k], "sub", shift(k)) for k in (1, 3, 2)]

    far_got = over_sub(far)

    mid, pair, other = pl.pallas_call(
        functools.partial(near_kernel, chunk),
        in_specs=[SMEM, SMEM, SMEM, VMEM] + [ANY] * 3,
        out_specs=[VMEM] * 3,
        out_shape=[struct((per_dev, 2, 8, 128))] * 3,
        scratch_shapes=[pltpu.VMEM(efie_near.shape, BF16)] * 2
        + [pltpu.VMEM((3 * per_dev, 2, 8, 128), F32), pltpu.SemaphoreType.DMA((2, steps))],
        compiler_params=params,
        cost_estimate=pl.CostEstimate(flops=200_000_000, bytes_accessed=4_600_000, transcendentals=0),
        name="near",
    )(me_ref, base, *in_hbm(near_cols.T, x, efie_near, dual_near), far[0])
    count = lax.axis_size("cluster")
    within = [(i, i ^ 1) for i in range(count)]
    between = [(i, i + 1) for i in range(1, count - 1, 2)] + [(i + 1, i) for i in range(1, count - 1, 2)]
    got_pair = lax.ppermute(pair, "cluster", within)
    got_other = lax.ppermute(other, "cluster", between)

    cols = far_cols.reshape(-1)
    owner = cols // per_dev
    earlier = (owner[:, None] == owner[None, :]) & (jnp.arange(128)[None, :] < jnp.arange(128)[:, None])
    order = jnp.sum(earlier.astype(jnp.int32), axis=1)
    slot = jnp.broadcast_to((turn(owner) * 4 + order)[None, :], (8, 128))
    place = jnp.broadcast_to((order * 16 + cols % per_dev)[:, None], (128, 128))
    sent = pl.pallas_call(
        send_kernel,
        in_specs=[VMEM] * 6,
        out_specs=VMEM,
        out_shape=struct((count * 17, 128)),
        compiler_params=small,
        name="send",
    )(slot, place, *far_got)
    sent, got_pair, got_other = pl.pallas_call(
        lambda *refs: None,
        in_specs=[ANY] * 3,
        out_specs=[ANY] * 3,
        out_shape=[struct((count * 17, 128)), struct(pair.shape), struct(pair.shape)],
        input_output_aliases={0: 0, 1: 1, 2: 2},
        compiler_params=small,
        name="join",
    )(sent, got_pair, got_other)
    near = pl.pallas_call(
        merge_kernel,
        in_specs=[VMEM] * 3,
        out_specs=[VMEM] * 4,
        out_shape=[struct((4, per_dev, 128))] * 4,
        compiler_params=small,
        name="merge",
    )(*(v.reshape(per_dev * 16, 128) for v in (mid, got_pair, got_other)))
    near_got = over_sub(near)
    path = sorted(range(count), key=turn)
    got = lax.all_to_all(sent.reshape(count * 17, 1, 128), "cluster", 0, 0, axis_index_groups=[path], tiled=True)
    efie, dual = pl.pallas_call(
        sum_kernel,
        in_specs=[VMEM] * 5,
        out_specs=[VMEM] * 2,
        out_shape=[struct((per_dev, 2, 128), BF16)] * 2,
        compiler_params=small,
        name="total",
    )(got.reshape(count * 17, 128), *near_got)
    shape = (per_dev, 2, 1, 128)
    return efie.reshape(shape), dual.reshape(shape)


def solution(mesh):
    return jax.shard_map(
        per_device,
        mesh=mesh,
        in_specs=(
            P("cluster", None, None, None),
            P("cluster", None, None, "sub", None),
            P("cluster", None, None, "sub", None),
            P("cluster", None, None, "sub", None),
            P("cluster", None, None, "sub", None),
            P("cluster", None),
            P("cluster", None),
            P("cluster", "sub", None, None, None),
            P("cluster", "sub", None, None, None),
            P("cluster", "sub"),
        ),
        out_specs=(P("cluster", None, "sub", None), P("cluster", None, "sub", None)),
        check_vma=False,
    )
```

```python
import functools

import jax
import jax.numpy as jnp
from jax import lax
from jax.experimental import pallas as pl
from jax.experimental.pallas import tpu as pltpu
from jax.sharding import PartitionSpec as P

F32 = jnp.float32
BF16 = jnp.bfloat16
MIB = 1024 * 1024


def iota(shape, dim):
    return lax.broadcasted_iota(jnp.int32, shape, dim)


def dot(left, right, dims=((1,), (0,))):
    return lax.dot_general(left, right, (dims, ((), ())), preferred_element_type=F32)


def vectors(x, me, cluster, copies):
    rows = 8 * copies
    shape = (2 * rows, x.shape[0])
    row, col = iota(shape, 0), iota(shape, 1)
    half = row // rows
    part = (row // copies) % 2
    vec = (me + (row % rows) // (2 * copies)) & 3
    wanted = cluster * 8 + jnp.where(half == part, 0, 1) * 4 + vec
    sign = jnp.where((half == 1) & (part == 1), -1.0, 1.0)
    both = dot(jnp.where(col == wanted, sign, 0.0).astype(BF16), x)
    return jnp.concatenate([both[:rows], both[rows:]], axis=1).astype(BF16)


def planes(ref, at, axis):
    return jnp.concatenate([ref[at, :, q].reshape(128, 128) for q in (0, 1)], axis=axis)


def far_kernel(chunk, me_ref, rank_ref, x_ref, le, re, ld, rd, *rest):
    *outs, ble, bre, bld, brd, lhs, sems = rest
    clusters = ble.shape[0]
    steps = clusters // chunk

    def loads(i):
        part = pl.ds(i * chunk, chunk)
        pairs = ((le, ble), (ld, bld), (re, bre), (rd, brd))
        return [pltpu.make_async_copy(a.at[part], b.at[part], sems.at[j, i]) for j, (a, b) in enumerate(pairs)]

    for i in range(steps):
        for copy in loads(i):
            copy.start()
    me = me_ref[0]
    x = x_ref[...]
    lane, sublane = iota((8, 128), 1), iota((8, 128), 0)
    for cluster in range(clusters):
        lhs[cluster] = vectors(x, me, cluster, 8)

    def spread(coef, keep):
        rows = [jnp.where(keep, coef[k * 8 : k * 8 + 8], 0.0) for k in range(8)]
        turned = [v for k in range(4) for v in (-rows[2 * k + 1], rows[2 * k])]
        both = [jnp.concatenate(rows, axis=0), jnp.concatenate(turned, axis=0)]
        return jnp.concatenate(both, axis=1).astype(BF16)

    def coefs(cluster):
        u = jnp.concatenate([planes(ble, cluster, 1), planes(bld, cluster, 1)], axis=0)
        return dot(lhs[cluster], u, ((1,), (1,)))

    def mixed(cluster, coef):
        ranks = jnp.zeros((8, 128), jnp.int32)
        for f in range(8):
            ranks = jnp.where(lane // 16 == f, rank_ref[f, cluster], ranks)
        keep = (lane // 16 == sublane) & (me * 16 + lane % 16 < ranks)
        return jnp.concatenate([spread(coef[:, :128], keep), spread(coef[:, 128:], keep)], axis=0)

    def results(cluster, mix):
        v = jnp.concatenate([planes(bre, cluster, 0), planes(brd, cluster, 0)], axis=1)
        far = dot(mix, v)
        for op in range(2):
            for k in range(4):
                for q in range(2):
                    start = op * 64 + k * 16 + q * 8
                    outs[k][op * 2 + q, cluster * 8 : cluster * 8 + 8, :] = far[
                        start : start + 8, op * 128 : op * 128 + 128
                    ]

    for i in range(steps):
        copies = loads(i)
        these = range(i * chunk, i * chunk + chunk)
        for copy in copies[:2]:
            copy.wait()
        coef = [coefs(cluster) for cluster in these]
        mix = [mixed(cluster, c) for cluster, c in zip(these, coef)]
        for copy in copies[2:]:
            copy.wait()
        for cluster, m in zip(these, mix):
            results(cluster, m)

def near_kernel(chunk, me_ref, base_ref, col_ref, x_ref, de, dd, after, mid, pair, other, bde, bdd, window, sems):
    clusters = bde.shape[0]
    steps = clusters // chunk

    def loads(i):
        part = pl.ds(i * chunk, chunk)
        pairs = ((de, bde), (dd, bdd))
        return [pltpu.make_async_copy(a.at[part], b.at[part], sems.at[j, i]) for j, (a, b) in enumerate(pairs)]

    for i in range(steps):
        for copy in loads(i):
            copy.start()
    me, base = me_ref[0], base_ref[0]
    x = x_ref[...]
    window[...] = jnp.zeros_like(window)
    lhs = [vectors(x, me, cluster, 1) for cluster in range(clusters)]
    for i in range(steps):
        for copy in loads(i):
            copy.wait()
        these = [(cluster, slot) for cluster in range(i * chunk, i * chunk + chunk) for slot in range(2)]
        outs = []
        for cluster, slot in these:
            d = jnp.concatenate([r[cluster, slot].reshape(256, 128) for r in (bde, bdd)], axis=1)
            outs.append(dot(lhs[cluster], d))
        for (cluster, slot), out in zip(these, outs):
            target = col_ref[slot, cluster] - base
            window[target, 0] += out[:, :128]
            window[target, 1] += out[:, 128:]
    odd = (base // 16) & 1 == 0
    mid[...] = window[16:32]
    pair[...] = window[pl.ds(jnp.where(odd, 0, 32), 16)]
    other[...] = window[pl.ds(jnp.where(odd, 32, 0), 16)]


def halves(value):
    high = value.astype(BF16)
    return high, (value - high.astype(F32)).astype(BF16)


def send_kernel(slot_ref, cols_ref, a, b, c, d, out):
    slot = jnp.broadcast_to(slot_ref[0:1, :], (64, 128))
    target = iota((64, 128), 0)
    picks = [jnp.where(slot == target * 4 + k, 1.0, 0.0).astype(BF16) for k in range(4)]
    pick = jnp.concatenate(picks, axis=0)
    pick = jnp.concatenate([pick, pick], axis=1)
    for half in range(2):
        parts = []
        for j in (half * 2, half * 2 + 1):
            high, low = halves(a[j] + b[j] + c[j] + d[j])
            parts.append(jnp.concatenate([high, low], axis=0))
        moved = dot(pick, jnp.concatenate(parts, axis=1))
        for q in range(2):
            for k in range(4):
                rows = pl.ds(k * 4 + half * 2 + q, 64, stride=17)
                out[rows, :] = moved[k * 64 : k * 64 + 64, q * 128 : q * 128 + 128]
    here = jnp.where(slot // 4 == target, 1.0, 0.0).astype(BF16)
    place = jnp.where(cols_ref[...] == iota((128, 128), 1), 1.0, 0.0).astype(BF16)
    out[pl.ds(16, 64, stride=17), :] = dot(here, place)


def merge_kernel(mid, pair, other, *near):
    for k in range(4):
        for j in range(4):
            rows = pl.ds((j // 2) * 8 + k * 2 + j % 2, 16, stride=16)
            near[k][j] = mid[rows, :] + pair[rows, :] + other[rows, :]


def sum_kernel(got, na, nb, nc, nd, efie, dual):
    marks = got[pl.ds(16, 64, stride=17), :].T
    pick = jnp.concatenate([marks[k * 16 : k * 16 + 16, :] for k in range(4)], axis=1).astype(BF16)
    pick = jnp.concatenate([pick, pick], axis=1)
    sums = []
    for j in range(4):
        value = jnp.concatenate([got[pl.ds(k * 4 + j, 64, stride=17), :] for k in range(4)], axis=0)
        high, low = halves(value)
        far = dot(pick, jnp.concatenate([high, low], axis=0))
        sums.append(far + na[j] + nb[j] + nc[j] + nd[j])
    efie[...] = jnp.stack([sums[0], sums[1]], axis=1).astype(BF16)
    dual[...] = jnp.stack([sums[2], sums[3]], axis=1).astype(BF16)


def turn(index):
    z, y, core = index // 8, (index // 2) % 4, index % 2
    return 63 - z * 8 - (y + (z % 2) * (3 - 2 * y)) * 2 - (core + (y % 2) * (1 - 2 * core))


SMEM = pl.BlockSpec(memory_space=pltpu.SMEM)
VMEM = pl.BlockSpec(memory_space=pltpu.VMEM)
ANY = pl.BlockSpec(memory_space=pl.ANY)


def per_device(
    adjoint_input,
    efie_left,
    efie_right,
    dual_left,
    dual_right,
    block_ranks,
    far_cols,
    efie_near,
    dual_near,
    near_cols,
):
    per_dev = adjoint_input.shape[0]
    subs = lax.axis_size("sub")
    position = lax.axis_index("cluster")
    me = lax.axis_index("sub")
    me_ref = me.astype(jnp.int32).reshape(1)
    base = (position * per_dev - per_dev).astype(jnp.int32).reshape(1)
    x = adjoint_input.reshape(per_dev * 8, 128)
    params = pltpu.CompilerParams(vmem_limit_bytes=24 * MIB)
    small = pltpu.CompilerParams(vmem_limit_bytes=12 * MIB)

    def struct(shape, dtype=F32):
        return jax.ShapeDtypeStruct(shape, dtype)

    def in_hbm(*values):
        return [pltpu.with_memory_space_constraint(v, pltpu.HBM) for v in values]

    chunk = 8
    steps = per_dev // chunk
    far = pl.pallas_call(
        functools.partial(far_kernel, chunk),
        in_specs=[SMEM, SMEM, VMEM] + [ANY] * 4,
        out_specs=[VMEM] * 4,
        out_shape=[struct((4, 128, 128), F32)] * 4,
        scratch_shapes=[pltpu.VMEM(efie_left.shape, BF16)] * 4
        + [pltpu.VMEM((per_dev, 64, 256), BF16), pltpu.SemaphoreType.DMA((4, steps))],
        compiler_params=params,
        cost_estimate=pl.CostEstimate(flops=200_000_000, bytes_accessed=5_300_000, transcendentals=0),
        name="far",
    )(me_ref, *in_hbm(block_ranks.T, x, efie_left, efie_right, dual_left, dual_right))

    def shift(k):
        return [(i, (i + k) % subs) for i in range(subs)]

    def over_sub(parts):
        return [parts[0]] + [lax.ppermute(parts[k], "sub", shift(k)) for k in (1, 3, 2)]

    far_got = over_sub(far)

    mid, pair, other = pl.pallas_call(
        functools.partial(near_kernel, chunk),
        in_specs=[SMEM, SMEM, SMEM, VMEM] + [ANY] * 3,
        out_specs=[VMEM] * 3,
        out_shape=[struct((per_dev, 2, 8, 128))] * 3,
        scratch_shapes=[pltpu.VMEM(efie_near.shape, BF16)] * 2
        + [pltpu.VMEM((3 * per_dev, 2, 8, 128), F32), pltpu.SemaphoreType.DMA((2, steps))],
        compiler_params=params,
        cost_estimate=pl.CostEstimate(flops=200_000_000, bytes_accessed=4_600_000, transcendentals=0),
        name="near",
    )(me_ref, base, *in_hbm(near_cols.T, x, efie_near, dual_near), far[0])
    count = lax.axis_size("cluster")
    within = [(i, i ^ 1) for i in range(count)]
    between = [(i, i + 1) for i in range(1, count - 1, 2)] + [(i + 1, i) for i in range(1, count - 1, 2)]
    got_other = lax.ppermute(other, "cluster", between)
    got_pair = lax.ppermute(pair, "cluster", within)

    cols = far_cols.reshape(-1)
    owner = cols // per_dev
    earlier = (owner[:, None] == owner[None, :]) & (jnp.arange(128)[None, :] < jnp.arange(128)[:, None])
    order = jnp.sum(earlier.astype(jnp.int32), axis=1)
    slot = jnp.broadcast_to((turn(owner) * 4 + order)[None, :], (8, 128))
    place = jnp.broadcast_to((order * 16 + cols % per_dev)[:, None], (128, 128))
    sent = pl.pallas_call(
        send_kernel,
        in_specs=[VMEM] * 6,
        out_specs=VMEM,
        out_shape=struct((count * 17, 128)),
        compiler_params=small,
        name="send",
    )(slot, place, *far_got)
    sent, got_other, got_pair = pl.pallas_call(
        lambda *refs: None,
        in_specs=[ANY] * 3,
        out_specs=[ANY] * 3,
        out_shape=[struct((count * 17, 128)), struct(pair.shape), struct(pair.shape)],
        input_output_aliases={0: 0, 1: 1, 2: 2},
        compiler_params=small,
        name="join",
    )(sent, got_other, got_pair)
    near = pl.pallas_call(
        merge_kernel,
        in_specs=[VMEM] * 3,
        out_specs=[VMEM] * 4,
        out_shape=[struct((4, per_dev, 128))] * 4,
        compiler_params=small,
        name="merge",
    )(*(v.reshape(per_dev * 16, 128) for v in (mid, got_pair, got_other)))
    near_got = over_sub(near)
    path = sorted(range(count), key=turn)
    got = lax.all_to_all(sent.reshape(count * 17, 1, 128), "cluster", 0, 0, axis_index_groups=[path], tiled=True)
    efie, dual = pl.pallas_call(
        sum_kernel,
        in_specs=[VMEM] * 5,
        out_specs=[VMEM] * 2,
        out_shape=[struct((per_dev, 2, 128), BF16)] * 2,
        compiler_params=small,
        name="total",
    )(got.reshape(count * 17, 128), *near_got)
    shape = (per_dev, 2, 1, 128)
    return efie.reshape(shape), dual.reshape(shape)


def solution(mesh):
    return jax.shard_map(
        per_device,
        mesh=mesh,
        in_specs=(
            P("cluster", None, None, None),
            P("cluster", None, None, "sub", None),
            P("cluster", None, None, "sub", None),
            P("cluster", None, None, "sub", None),
            P("cluster", None, None, "sub", None),
            P("cluster", None),
            P("cluster", None),
            P("cluster", "sub", None, None, None),
            P("cluster", "sub", None, None, None),
            P("cluster", "sub"),
        ),
        out_specs=(P("cluster", None, "sub", None), P("cluster", None, "sub", None)),
        check_vma=False,
    )
```

```python
import functools

import jax
import jax.numpy as jnp
from jax import lax
from jax.experimental import pallas as pl
from jax.experimental.pallas import tpu as pltpu
from jax.sharding import PartitionSpec as P

F32 = jnp.float32
BF16 = jnp.bfloat16
MIB = 1024 * 1024


def iota(shape, dim):
    return lax.broadcasted_iota(jnp.int32, shape, dim)


def dot(left, right, dims=((1,), (0,))):
    return lax.dot_general(left, right, (dims, ((), ())), preferred_element_type=F32)


def vectors(x, me, cluster, copies):
    rows = 8 * copies
    shape = (2 * rows, x.shape[0])
    row, col = iota(shape, 0), iota(shape, 1)
    half = row // rows
    part = (row // copies) % 2
    vec = (me + (row % rows) // (2 * copies)) & 3
    wanted = cluster * 8 + jnp.where(half == part, 0, 1) * 4 + vec
    sign = jnp.where((half == 1) & (part == 1), -1.0, 1.0)
    both = dot(jnp.where(col == wanted, sign, 0.0).astype(BF16), x)
    return jnp.concatenate([both[:rows], both[rows:]], axis=1).astype(BF16)


def planes(ref, at, axis):
    return jnp.concatenate([ref[at, :, q].reshape(128, 128) for q in (0, 1)], axis=axis)


def far_kernel(chunk, me_ref, rank_ref, x_ref, le, re, ld, rd, *rest):
    *outs, ble, bre, bld, brd, lhs, sems = rest
    clusters = ble.shape[0]
    steps = clusters // chunk

    def loads(i):
        part = pl.ds(i * chunk, chunk)
        pairs = ((le, ble), (ld, bld), (re, bre), (rd, brd))
        return [pltpu.make_async_copy(a.at[part], b.at[part], sems.at[j, i]) for j, (a, b) in enumerate(pairs)]

    for i in range(steps):
        for copy in loads(i):
            copy.start()
    me = me_ref[0]
    x = x_ref[...]
    lane, sublane = iota((8, 128), 1), iota((8, 128), 0)
    for cluster in range(clusters):
        lhs[cluster] = vectors(x, me, cluster, 8)

    def spread(coef, keep):
        rows = [jnp.where(keep, coef[k * 8 : k * 8 + 8], 0.0) for k in range(8)]
        turned = [v for k in range(4) for v in (-rows[2 * k + 1], rows[2 * k])]
        both = [jnp.concatenate(rows, axis=0), jnp.concatenate(turned, axis=0)]
        return jnp.concatenate(both, axis=1).astype(BF16)

    def coefs(cluster):
        u = jnp.concatenate([planes(ble, cluster, 1), planes(bld, cluster, 1)], axis=0)
        return dot(lhs[cluster], u, ((1,), (1,)))

    def mixed(cluster, coef):
        ranks = jnp.zeros((8, 128), jnp.int32)
        for f in range(8):
            ranks = jnp.where(lane // 16 == f, rank_ref[f, cluster], ranks)
        keep = (lane // 16 == sublane) & (me * 16 + lane % 16 < ranks)
        return jnp.concatenate([spread(coef[:, :128], keep), spread(coef[:, 128:], keep)], axis=0)

    def results(cluster, mix):
        v = jnp.concatenate([planes(bre, cluster, 0), planes(brd, cluster, 0)], axis=1)
        far = dot(mix, v)
        for op in range(2):
            for k in range(4):
                for q in range(2):
                    start = op * 64 + k * 16 + q * 8
                    outs[k][op * 2 + q, cluster * 8 : cluster * 8 + 8, :] = far[
                        start : start + 8, op * 128 : op * 128 + 128
                    ]

    for i in range(steps):
        copies = loads(i)
        these = range(i * chunk, i * chunk + chunk)
        for copy in copies[:2]:
            copy.wait()
        coef = [coefs(cluster) for cluster in these]
        mix = [mixed(cluster, c) for cluster, c in zip(these, coef)]
        for copy in copies[2:]:
            copy.wait()
        for cluster, m in zip(these, mix):
            results(cluster, m)

def near_kernel(chunk, me_ref, base_ref, col_ref, x_ref, de, dd, after, mid, pair, other, bde, bdd, window, sems):
    clusters = bde.shape[0]
    steps = clusters // chunk

    def loads(i):
        part = pl.ds(i * chunk, chunk)
        pairs = ((de, bde), (dd, bdd))
        return [pltpu.make_async_copy(a.at[part], b.at[part], sems.at[j, i]) for j, (a, b) in enumerate(pairs)]

    for i in range(steps):
        for copy in loads(i):
            copy.start()
    me, base = me_ref[0], base_ref[0]
    x = x_ref[...]
    window[...] = jnp.zeros_like(window)
    lhs = [vectors(x, me, cluster, 1) for cluster in range(clusters)]
    for i in range(steps):
        for copy in loads(i):
            copy.wait()
        these = [(cluster, slot) for cluster in range(i * chunk, i * chunk + chunk) for slot in range(2)]
        outs = []
        for cluster, slot in these:
            d = jnp.concatenate([r[cluster, slot].reshape(256, 128) for r in (bde, bdd)], axis=1)
            outs.append(dot(lhs[cluster], d))
        for (cluster, slot), out in zip(these, outs):
            target = col_ref[slot, cluster] - base
            window[target, 0] += out[:, :128]
            window[target, 1] += out[:, 128:]
    odd = (base // 16) & 1 == 0
    mid[...] = window[16:32]
    pair[...] = window[pl.ds(jnp.where(odd, 0, 32), 16)]
    other[...] = window[pl.ds(jnp.where(odd, 32, 0), 16)]


def halves(value):
    high = value.astype(BF16)
    return high, (value - high.astype(F32)).astype(BF16)


def send_kernel(slot_ref, cols_ref, a, b, c, d, out):
    slot = jnp.broadcast_to(slot_ref[0:1, :], (64, 128))
    target = iota((64, 128), 0)
    picks = [jnp.where(slot == target * 4 + k, 1.0, 0.0).astype(BF16) for k in range(4)]
    pick = jnp.concatenate(picks, axis=0)
    pick = jnp.concatenate([pick, pick], axis=1)
    for half in range(2):
        parts = []
        for j in (half * 2, half * 2 + 1):
            high, low = halves(a[j] + b[j] + c[j] + d[j])
            parts.append(jnp.concatenate([high, low], axis=0))
        moved = dot(pick, jnp.concatenate(parts, axis=1))
        for q in range(2):
            for k in range(4):
                rows = pl.ds(k * 4 + half * 2 + q, 64, stride=17)
                out[rows, :] = moved[k * 64 : k * 64 + 64, q * 128 : q * 128 + 128]
    here = jnp.where(slot // 4 == target, 1.0, 0.0).astype(BF16)
    place = jnp.where(cols_ref[...] == iota((128, 128), 1), 1.0, 0.0).astype(BF16)
    out[pl.ds(16, 64, stride=17), :] = dot(here, place)


def merge_kernel(mid, pair, other, *near):
    for k in range(4):
        for j in range(4):
            rows = pl.ds((j // 2) * 8 + k * 2 + j % 2, 16, stride=16)
            near[k][j] = mid[rows, :] + pair[rows, :] + other[rows, :]


def sum_kernel(got, na, nb, nc, nd, efie, dual):
    marks = got[pl.ds(16, 64, stride=17), :].T
    pick = jnp.concatenate([marks[k * 16 : k * 16 + 16, :] for k in range(4)], axis=1).astype(BF16)
    pick = jnp.concatenate([pick, pick], axis=1)
    parts = []
    for j in range(4):
        value = jnp.concatenate([got[pl.ds(k * 4 + j, 64, stride=17), :] for k in range(4)], axis=0)
        parts.append(jnp.concatenate(halves(value), axis=0))
    far = dot(pick, jnp.concatenate(parts, axis=1))
    sums = [far[:, j * 128 : j * 128 + 128] + na[j] + nb[j] + nc[j] + nd[j] for j in range(4)]
    efie[...] = jnp.stack([sums[0], sums[1]], axis=1).astype(BF16)
    dual[...] = jnp.stack([sums[2], sums[3]], axis=1).astype(BF16)


def turn(index):
    z, y, core = index // 8, (index // 2) % 4, index % 2
    return 63 - z * 8 - (y + (z % 2) * (3 - 2 * y)) * 2 - (core + (y % 2) * (1 - 2 * core))


SMEM = pl.BlockSpec(memory_space=pltpu.SMEM)
VMEM = pl.BlockSpec(memory_space=pltpu.VMEM)
ANY = pl.BlockSpec(memory_space=pl.ANY)


def per_device(
    adjoint_input,
    efie_left,
    efie_right,
    dual_left,
    dual_right,
    block_ranks,
    far_cols,
    efie_near,
    dual_near,
    near_cols,
):
    per_dev = adjoint_input.shape[0]
    subs = lax.axis_size("sub")
    position = lax.axis_index("cluster")
    me = lax.axis_index("sub")
    me_ref = me.astype(jnp.int32).reshape(1)
    base = (position * per_dev - per_dev).astype(jnp.int32).reshape(1)
    x = adjoint_input.reshape(per_dev * 8, 128)
    params = pltpu.CompilerParams(vmem_limit_bytes=24 * MIB)
    small = pltpu.CompilerParams(vmem_limit_bytes=12 * MIB)

    def struct(shape, dtype=F32):
        return jax.ShapeDtypeStruct(shape, dtype)

    def in_hbm(*values):
        return [pltpu.with_memory_space_constraint(v, pltpu.HBM) for v in values]

    chunk = 8
    steps = per_dev // chunk
    far = pl.pallas_call(
        functools.partial(far_kernel, chunk),
        in_specs=[SMEM, SMEM, VMEM] + [ANY] * 4,
        out_specs=[VMEM] * 4,
        out_shape=[struct((4, 128, 128), F32)] * 4,
        scratch_shapes=[pltpu.VMEM(efie_left.shape, BF16)] * 4
        + [pltpu.VMEM((per_dev, 64, 256), BF16), pltpu.SemaphoreType.DMA((4, steps))],
        compiler_params=params,
        cost_estimate=pl.CostEstimate(flops=200_000_000, bytes_accessed=5_300_000, transcendentals=0),
        name="far",
    )(me_ref, *in_hbm(block_ranks.T, x, efie_left, efie_right, dual_left, dual_right))

    def shift(k):
        return [(i, (i + k) % subs) for i in range(subs)]

    def over_sub(parts):
        return [parts[0]] + [lax.ppermute(parts[k], "sub", shift(k)) for k in (1, 3, 2)]

    far_got = over_sub(far)

    mid, pair, other = pl.pallas_call(
        functools.partial(near_kernel, chunk),
        in_specs=[SMEM, SMEM, SMEM, VMEM] + [ANY] * 3,
        out_specs=[VMEM] * 3,
        out_shape=[struct((per_dev, 2, 8, 128))] * 3,
        scratch_shapes=[pltpu.VMEM(efie_near.shape, BF16)] * 2
        + [pltpu.VMEM((3 * per_dev, 2, 8, 128), F32), pltpu.SemaphoreType.DMA((2, steps))],
        compiler_params=params,
        cost_estimate=pl.CostEstimate(flops=200_000_000, bytes_accessed=4_600_000, transcendentals=0),
        name="near",
    )(me_ref, base, *in_hbm(near_cols.T, x, efie_near, dual_near), far[0])
    count = lax.axis_size("cluster")
    within = [(i, i ^ 1) for i in range(count)]
    between = [(i, i + 1) for i in range(1, count - 1, 2)] + [(i + 1, i) for i in range(1, count - 1, 2)]
    got_other = lax.ppermute(other, "cluster", between)
    got_pair = lax.ppermute(pair, "cluster", within)

    cols = far_cols.reshape(-1)
    owner = cols // per_dev
    earlier = (owner[:, None] == owner[None, :]) & (jnp.arange(128)[None, :] < jnp.arange(128)[:, None])
    order = jnp.sum(earlier.astype(jnp.int32), axis=1)
    slot = jnp.broadcast_to((turn(owner) * 4 + order)[None, :], (8, 128))
    place = jnp.broadcast_to((order * 16 + cols % per_dev)[:, None], (128, 128))
    sent = pl.pallas_call(
        send_kernel,
        in_specs=[VMEM] * 6,
        out_specs=VMEM,
        out_shape=struct((count * 17, 128)),
        compiler_params=small,
        name="send",
    )(slot, place, *far_got)
    sent, got_other, got_pair = pl.pallas_call(
        lambda *refs: None,
        in_specs=[ANY] * 3,
        out_specs=[ANY] * 3,
        out_shape=[struct((count * 17, 128)), struct(pair.shape), struct(pair.shape)],
        input_output_aliases={0: 0, 1: 1, 2: 2},
        compiler_params=small,
        name="join",
    )(sent, got_other, got_pair)
    near = pl.pallas_call(
        merge_kernel,
        in_specs=[VMEM] * 3,
        out_specs=[VMEM] * 4,
        out_shape=[struct((4, per_dev, 128))] * 4,
        compiler_params=small,
        name="merge",
    )(*(v.reshape(per_dev * 16, 128) for v in (mid, got_pair, got_other)))
    near_got = over_sub(near)
    path = sorted(range(count), key=turn)
    got = lax.all_to_all(sent.reshape(count * 17, 1, 128), "cluster", 0, 0, axis_index_groups=[path], tiled=True)
    efie, dual = pl.pallas_call(
        sum_kernel,
        in_specs=[VMEM] * 5,
        out_specs=[VMEM] * 2,
        out_shape=[struct((per_dev, 2, 128), BF16)] * 2,
        compiler_params=small,
        name="total",
    )(got.reshape(count * 17, 128), *near_got)
    shape = (per_dev, 2, 1, 128)
    return efie.reshape(shape), dual.reshape(shape)


def solution(mesh):
    return jax.shard_map(
        per_device,
        mesh=mesh,
        in_specs=(
            P("cluster", None, None, None),
            P("cluster", None, None, "sub", None),
            P("cluster", None, None, "sub", None),
            P("cluster", None, None, "sub", None),
            P("cluster", None, None, "sub", None),
            P("cluster", None),
            P("cluster", None),
            P("cluster", "sub", None, None, None),
            P("cluster", "sub", None, None, None),
            P("cluster", "sub"),
        ),
        out_specs=(P("cluster", None, "sub", None), P("cluster", None, "sub", None)),
        check_vma=False,
    )
```
